256 devices in a mesh: seq: 64 (over x_lo, z, y), rep: 4 (over x_hi, core).
Axes of the slice: x: 4 (x_hi: 2, x_lo: 2; x = x_hi * 2 + x_lo), y: 4, z: 8, core: 2. Of those that a mesh axis runs over, the one named last changes fastest.
Arguments:
- queries: bfloat16 [32768, 4096], P('seq', 'rep'), may hold values from -12 to 12
- keys: bfloat16 [32768, 1024], P('seq', 'rep'), may hold values from -6 to 6
- values: bfloat16 [32768, 1024], P('seq', 'rep'), may hold values from -6 to 6
- output_gradient: bfloat16 [32768, 4096], P('seq'), may hold values from -6 to 6
- output_weight: bfloat16 [4096, 4096], P('rep'), may hold values from -0.09375 to 0.09375
- adapter_down: bfloat16 [4096, 32], P('rep'), may hold values from -0.09375 to 0.09375
- adapter_up: bfloat16 [32, 4096], replicated, may hold values from -0.09375 to 0.09375
- positions: int32 [32768], P('seq'), may hold values from 0 to 32767, as said below
- block_pair_mask: int32 [64, 2, 2, 2], P('seq'), may hold values from 0 to 2, as said below
Outputs:
- query_gradient: bfloat16 [32768, 4096], P('seq', 'rep')
- key_gradient: bfloat16 [32768, 1024], P('seq', 'rep')
- value_gradient: bfloat16 [32768, 1024], P('seq', 'rep')
- adapter_down_gradient: float32 [4096, 32], P('rep')
- adapter_up_gradient: float32 [32, 4096], replicated
The draws below stay inside these ranges and needn't reach their ends.
Inputs may be any that keep to these rules, and one draw needn't show every extreme that they name: The sequence is cut into blocks of 256 consecutive positions, and each device holds two such blocks, in a drawn order; every position occurs once. block_pair_mask[d, 0, a, a] = 2; every other entry is 1 where all positions of the key half precede those of the query half, and 0 where all follow.
All inputs are finite; a program needn't handle non-finite values.
Results may differ from the reference program's by a relative error of at most 0.017.
Values may be sent and summed in bfloat16 or wider, within the bound.
A program may use at most 128 MiB of HBM per device.

```python
import jax
import jax.numpy as jnp
from jax import lax

MODEL_WIDTH = 4096
QUERY_HEADS = 32
KV_HEADS = 8
HEAD_SIZE = 128
ADAPTER_RANK = 32
TOK_DEV = 512
HALF = 256
TOKENS = 32768
N_SEQ = 64


def span_order(key):
    return jax.random.permutation(jax.random.fold_in(key, 7), TOKENS // HALF).astype(jnp.int32)


def drawn_rows(key):
    return jax.random.bernoulli(jax.random.fold_in(key, 5), 0.04, (TOKENS,))


def key_field(key, boost):
    shape = (TOKENS, KV_HEADS * HEAD_SIZE)
    raw = jnp.clip(jax.random.normal(jax.random.fold_in(key, 21), shape, jnp.float32), -6.0, 6.0)
    base = raw
    lift = jnp.where(drawn_rows(key), boost, 1.0)
    return base * lift[:, None]


def draw_positions(key, part):
    order = span_order(key)
    slot = jnp.arange(TOKENS, dtype=jnp.int32)
    return (order[slot // HALF] * HALF + slot % HALF).astype(jnp.int32)


def draw_block_pair_mask(key, part):
    order = span_order(key)
    mine = order.reshape(TOKENS // TOK_DEV, 2)
    prev = jnp.roll(mine, 1, axis=0)
    step_own = jnp.where(mine[:, None, :] < mine[:, :, None], 1, 0)
    diagonal = jnp.eye(2, dtype=jnp.int32) == 1
    step_own = jnp.where(diagonal[None], 2, step_own)
    step_prev = jnp.where(prev[:, None, :] < mine[:, :, None], 1, 0)
    return jnp.stack([step_own, step_prev], axis=1).astype(jnp.int32)


def draw_keys(key, part):
    field = key_field(key, 1.0)
    return field.astype(jnp.bfloat16)


def draw_queries(key, part):
    shape = (TOKENS, QUERY_HEADS * HEAD_SIZE)
    key = jax.random.fold_in(key, 3)
    result = jnp.clip(jax.random.normal(key, shape, jnp.float32), -6.0, 6.0)
    return result.astype(jnp.bfloat16)


def block_scale(own_key, dims, pieces, smallest, high):
    def one(axis_at, parts):
        draws = jax.random.uniform(jax.random.fold_in(jax.random.fold_in(own_key, 6), axis_at), (parts,), jnp.float32, smallest / len(pieces), high / len(pieces))
        return jnp.repeat(jnp.exp(draws), dims[axis_at] // parts).reshape((-1,) + (1,) * (len(dims) - axis_at - 1))

    level = one(*pieces[0])
    for cut in pieces[1:]:
        level = level * one(*cut)
    return level


def bell_draw(rng, dims, scale, bound, split=(), kind=jnp.bfloat16):
    entries = scale * jax.random.normal(rng, dims, jnp.float32)
    if split:
        entries = entries * block_scale(rng, dims, split, -0.22, 0.18)
    return jnp.clip(entries, -bound, bound).astype(kind)


def setup_inputs(seed: int = 0) -> dict:
    splits = jax.random.split(jax.random.key(seed), 10)
    queries = draw_queries(jax.random.fold_in(splits[9], 71), 0)
    keys = draw_keys(jax.random.fold_in(splits[9], 71), 0)
    values = bell_draw(splits[2], (TOKENS, KV_HEADS * HEAD_SIZE), 1.0, 6.0, ((0, 64), (1, 4)))
    output_gradient = bell_draw(splits[3], (TOKENS, MODEL_WIDTH), 1.0, 6.0, ((0, 64),))
    output_weight = bell_draw(splits[4], (QUERY_HEADS * HEAD_SIZE, MODEL_WIDTH), (QUERY_HEADS * HEAD_SIZE) ** -0.5, 0.09375, ((0, 4),))
    adapter_down = bell_draw(splits[5], (QUERY_HEADS * HEAD_SIZE, ADAPTER_RANK), (QUERY_HEADS * HEAD_SIZE) ** -0.5, 0.09375, ((0, 4),))
    adapter_up = bell_draw(splits[6], (ADAPTER_RANK, MODEL_WIDTH), MODEL_WIDTH ** -0.5, 0.09375)
    positions = draw_positions(jax.random.fold_in(splits[9], 71), 0)
    block_pair_mask = draw_block_pair_mask(jax.random.fold_in(splits[9], 71), 0)
    return dict(queries=queries, keys=keys, values=values, output_gradient=output_gradient, output_weight=output_weight, adapter_down=adapter_down, adapter_up=adapter_up, positions=positions, block_pair_mask=block_pair_mask)


def angles(pos, width):
    freq = 1000000.0 ** (-(jnp.arange(width // 2).astype(jnp.float32) * 2.0 / width))
    phase = pos.astype(jnp.float32)[:, None] * freq[None, :]
    return jnp.cos(phase), jnp.sin(phase)


def rotate(x, cosine, sine):
    half_w = x.shape[-1] // 2
    first, second = x[..., :half_w], x[..., half_w:]
    c_term, s_term = cosine[:, None, :], sine[:, None, :]
    return jnp.concatenate([first * c_term - second * s_term, second * c_term + first * s_term], -1)


def unrotate(x, cosine, sine):
    half_w = x.shape[-1] // 2
    first, second = x[..., :half_w], x[..., half_w:]
    c_term, s_term = cosine[:, None, :], sine[:, None, :]
    return jnp.concatenate([first * c_term + second * s_term, second * c_term - first * s_term], -1)


def tile_modes(modes, half_rows):
    return jnp.broadcast_to(modes[:, None, :, None], (2, half_rows, 2, half_rows)).reshape(2 * half_rows, 2 * half_rows)


def scores(q_rot, k_rot, allowed):
    raw = jnp.einsum("tkgw,ukw->kgtu", q_rot.astype(jnp.float32), k_rot.astype(jnp.float32))
    raw = raw * (q_rot.shape[-1] ** -0.5)
    return jnp.where(allowed[None, None], raw, -jnp.inf)


def step_back(s_block, lse, q_rot, k_rot, v_blk, attention_gradient, delta):
    scale = q_rot.shape[-1] ** -0.5
    p_wide = jnp.exp(s_block - lse[..., None])
    p_narrow = p_wide.astype(jnp.bfloat16)
    d_prob = jnp.einsum("tkgw,ukw->kgtu", attention_gradient.astype(jnp.float32), v_blk.astype(jnp.float32))
    d_score = (p_wide * (d_prob - delta[..., None])).astype(jnp.bfloat16)
    dq_part = jnp.einsum("kgtu,ukw->tkgw", d_score.astype(jnp.float32), k_rot.astype(jnp.float32)) * scale
    dk_part = jnp.einsum("kgtu,tkgw->ukw", d_score.astype(jnp.float32), q_rot.astype(jnp.float32)) * scale
    dv_part = jnp.einsum("kgtu,tkgw->ukw", p_narrow.astype(jnp.float32), attention_gradient.astype(jnp.float32))
    return dq_part, dk_part, dv_part


def narrowed(x):
    return lax.optimization_barrier(x.astype(jnp.bfloat16)).astype(jnp.float32)


def reference(queries, keys, values, output_gradient, output_weight, adapter_down, adapter_up, positions, block_pair_mask):
    groups = QUERY_HEADS // KV_HEADS
    half_rows = TOK_DEV // 2
    q_blocks = queries.reshape(N_SEQ, TOK_DEV, QUERY_HEADS, HEAD_SIZE)
    k_blocks = keys.reshape(N_SEQ, TOK_DEV, KV_HEADS, HEAD_SIZE)
    v_blocks = values.reshape(N_SEQ, TOK_DEV, KV_HEADS, HEAD_SIZE)
    p_blocks = positions.reshape(N_SEQ, TOK_DEV)

    def prepare(item):
        q_one, k_one, pos = item
        cosine, sine = angles(pos, HEAD_SIZE)
        q_rot = rotate(q_one.astype(jnp.float32), cosine, sine).astype(jnp.bfloat16)
        k_rot = rotate(k_one.astype(jnp.float32), cosine, sine).astype(jnp.bfloat16)
        return q_rot.reshape(TOK_DEV, KV_HEADS, groups, HEAD_SIZE), k_rot

    q_rots, k_rots = lax.map(prepare, (q_blocks, k_blocks, p_blocks))
    k_prevs = jnp.roll(k_rots, 1, axis=0)
    v_prevs = jnp.roll(v_blocks, 1, axis=0)

    def masks(modes, pos):
        own_code = tile_modes(modes[0], half_rows)
        prev_code = tile_modes(modes[1], half_rows)
        own_allowed = (own_code == 1) | ((own_code == 2) & (pos[None, :] <= pos[:, None]))
        return own_allowed, prev_code == 1

    def forward(item):
        q_rot, k_rot, k_prev, v_own, v_prev, pos, modes = item
        own_allowed, prev_allowed = masks(modes, pos)
        s_own = scores(q_rot, k_rot, own_allowed)
        s_prev = scores(q_rot, k_prev, prev_allowed)
        lse = jnp.logaddexp(jax.nn.logsumexp(s_own, -1), jax.nn.logsumexp(s_prev, -1))
        p_own = jnp.exp(s_own - lse[..., None]).astype(jnp.bfloat16)
        p_prev = jnp.exp(s_prev - lse[..., None]).astype(jnp.bfloat16)
        attention_output = jnp.einsum("kgtu,ukw->tkgw", p_own.astype(jnp.float32), v_own.astype(jnp.float32))
        attention_output = attention_output + jnp.einsum("kgtu,ukw->tkgw", p_prev.astype(jnp.float32), v_prev.astype(jnp.float32))
        return attention_output.astype(jnp.bfloat16), lse

    attn_blocks, lse_blocks = lax.map(forward, (q_rots, k_rots, k_prevs, v_blocks, v_prevs, p_blocks, block_pair_mask))
    attention_gathered = attn_blocks.reshape(TOKENS, QUERY_HEADS * HEAD_SIZE)
    adapter_middle = jnp.dot(attention_gathered, adapter_down, preferred_element_type=jnp.float32).astype(jnp.bfloat16)
    backward_result = jnp.dot(output_gradient, adapter_up.T, preferred_element_type=jnp.float32).astype(jnp.bfloat16)
    adapter_down_gradient = 2.0 * jnp.dot(attention_gathered.T, backward_result, preferred_element_type=jnp.float32)
    adapter_up_gradient = 2.0 * jnp.dot(adapter_middle.T, output_gradient, preferred_element_type=jnp.float32)
    attention_gradient = jnp.dot(output_gradient, output_weight.T, preferred_element_type=jnp.float32)
    attention_gradient = (attention_gradient + 2.0 * jnp.dot(backward_result, adapter_down.T, preferred_element_type=jnp.float32)).astype(jnp.bfloat16)
    d_blocks = attention_gradient.reshape(N_SEQ, TOK_DEV, KV_HEADS, groups, HEAD_SIZE)

    def backward(item):
        q_rot, k_rot, k_prev, v_own, v_prev, pos, modes, lse, attention_output, d_one = item
        own_allowed, prev_allowed = masks(modes, pos)
        s_own = scores(q_rot, k_rot, own_allowed)
        s_prev = scores(q_rot, k_prev, prev_allowed)
        delta = jnp.sum(d_one.astype(jnp.float32) * attention_output.astype(jnp.float32), -1).transpose(1, 2, 0)
        dq_own, dk_own, dv_own = step_back(s_own, lse, q_rot, k_rot, v_own, d_one, delta)
        dq_prev, dk_prev, dv_prev = step_back(s_prev, lse, q_rot, k_prev, v_prev, d_one, delta)
        cosine, sine = angles(pos, HEAD_SIZE)
        dq_rot = (dq_own + dq_prev).reshape(TOK_DEV, QUERY_HEADS, HEAD_SIZE)
        q_grad = unrotate(dq_rot, cosine, sine).astype(jnp.bfloat16).reshape(TOK_DEV, QUERY_HEADS * HEAD_SIZE)
        return q_grad, dk_own, dv_own, narrowed(dk_prev), narrowed(dv_prev)

    q_grads, dk_own, dv_own, dk_prev, dv_prev = lax.map(backward, (q_rots, k_rots, k_prevs, v_blocks, v_prevs, p_blocks, block_pair_mask, lse_blocks, attn_blocks, d_blocks))
    dk_total = (dk_own + jnp.roll(dk_prev, -1, axis=0)).reshape(TOKENS, KV_HEADS, HEAD_SIZE)
    dv_total = dv_own + jnp.roll(dv_prev, -1, axis=0)
    cos_all, sin_all = angles(positions, HEAD_SIZE)
    key_gradient = unrotate(dk_total, cos_all, sin_all).astype(jnp.bfloat16).reshape(TOKENS, KV_HEADS * HEAD_SIZE)
    value_gradient = dv_total.astype(jnp.bfloat16).reshape(TOKENS, KV_HEADS * HEAD_SIZE)
    query_gradient = q_grads.reshape(TOKENS, QUERY_HEADS * HEAD_SIZE)
    return (query_gradient, key_gradient, value_gradient, adapter_down_gradient, adapter_up_gradient)
```

```python
import jax
import jax.numpy as jnp
from jax import lax
from jax.experimental import pallas as pl
from jax.experimental.pallas import tpu as pltpu
from jax.sharding import PartitionSpec as P

HEAD_SIZE = 128
MESH = pl.DeviceIdType.MESH
F32 = jnp.float32


def seq_at(j, z):
    return (j // 4) * 32 + z * 4 + j % 4


def sum_kernel(a_ref, b_ref, a_out, b_out, part, rs1, red1, rs2, ag1, full, b_all, ss, r1, r2, g1, g2, g3):
    s, r = lax.axis_index("seq"), lax.axis_index("rep")
    z, j = (s // 4) % 8, (s // 32) * 4 + s % 4
    along_z = [seq_at(j, (z + o) % 8) for o in range(8)]
    along_j = [seq_at((j + o) % 8, z) for o in range(8)]
    along_r = [(r + o) % 4 for o in range(4)]
    peers = [(p, r) for p in along_z[1:] + along_j[1:]] + [(s, p) for p in along_r[1:]]

    barrier = pltpu.get_barrier_semaphore()
    for p in peers:
        pl.semaphore_signal(barrier, inc=1, device_id=p, device_id_type=MESH)
    for c in range(8):
        part[c, 0:32, :] = a_ref[:, c * 128 : c * 128 + 128]
        part[c, 32:64, :] = b_ref[:, c * 128 : c * 128 + 128]
    pl.semaphore_wait(barrier, len(peers))

    def send(src, dst, k, sems, at):
        copy = pltpu.make_async_remote_copy(
            src_ref=src, dst_ref=dst, send_sem=ss.at[k], recv_sem=sems, device_id=at, device_id_type=MESH
        )
        copy.start()
        return copy

    copies = [
        send(part.at[(z + o) % 8], rs1.at[o], o, r1.at[o], (along_z[o], r)) for o in range(1, 8)
    ]
    total = part[z]
    for o in range(1, 8):
        copies[o - 1].wait()
        total = total + rs1[o]
    red1[...] = total.reshape(8, 8, 128)
    copies = [
        send(red1.at[(j + o) % 8], rs2.at[o], o, r2.at[o], (along_j[o], r)) for o in range(1, 8)
    ]
    total = red1[j]
    for o in range(1, 8):
        copies[o - 1].wait()
        total = total + rs2[o]
    ag1[j] = 2.0 * total
    copies = [send(ag1.at[j], ag1.at[j], o, g1.at[o], (along_j[o], r)) for o in range(1, 8)]
    for copy in copies:
        copy.wait()
    full[z] = ag1[...].reshape(64, 128)
    copies = [send(full.at[z], full.at[z], o, g2.at[o], (along_z[o], r)) for o in range(1, 8)]
    for copy in copies:
        copy.wait()
    b_all[r] = full[:, 32:64, :]
    copies = [send(b_all.at[r], b_all.at[r], o, g3.at[o], (s, along_r[o])) for o in range(1, 4)]
    for c in range(8):
        a_out[:, c * 128 : c * 128 + 128] = full[c, 0:32, :]
    for copy in copies:
        copy.wait()
    for q in range(4):
        for c in range(8):
            at = q * 1024 + c * 128
            b_out[:, at : at + 128] = b_all[q, c]


def adapter_sums(a, b):
    vmem = pl.BlockSpec(memory_space=pltpu.VMEM)
    dma = pltpu.SemaphoreType.DMA((8,))
    return pl.pallas_call(
        sum_kernel,
        out_shape=(jax.ShapeDtypeStruct((32, 1024), F32), jax.ShapeDtypeStruct((32, 4096), F32)),
        in_specs=[vmem, vmem],
        out_specs=(vmem, vmem),
        scratch_shapes=[
            pltpu.VMEM((8, 64, 128), F32),
            pltpu.VMEM((8, 64, 128), F32),
            pltpu.VMEM((8, 8, 128), F32),
            pltpu.VMEM((8, 8, 128), F32),
            pltpu.VMEM((8, 8, 128), F32),
            pltpu.VMEM((8, 64, 128), F32),
            pltpu.VMEM((4, 8, 32, 128), F32),
            dma, dma, dma, dma, dma, dma,
        ],
        compiler_params=pltpu.CompilerParams(collective_id=0, has_side_effects=True),
    )(a, b)


def shifted(x, axis, by):
    size = lax.axis_size(axis)
    return lax.ppermute(x, axis, [(i, (i + by) % size) for i in range(size)])


def angles(pos, width):
    freq = 1000000.0 ** (-(jnp.arange(width // 2).astype(jnp.float32) * 2.0 / width))
    phase = pos.astype(jnp.float32)[:, None] * freq[None, :]
    return (jnp.cos(phase), jnp.sin(phase))


def rotate(x, cosine, sine):
    half_w = x.shape[-1] // 2
    first, second = (x[..., :half_w], x[..., half_w:])
    c_term, s_term = (cosine[:, None, :], sine[:, None, :])
    return jnp.concatenate([first * c_term - second * s_term, second * c_term + first * s_term], -1)


def unrotate(x, cosine, sine):
    half_w = x.shape[-1] // 2
    first, second = (x[..., :half_w], x[..., half_w:])
    c_term, s_term = (cosine[:, None, :], sine[:, None, :])
    return jnp.concatenate([first * c_term + second * s_term, second * c_term - first * s_term], -1)


def tile_modes(modes, half_rows):
    return jnp.broadcast_to(modes[:, None, :, None], (2, half_rows, 2, half_rows)).reshape(
        2 * half_rows, 2 * half_rows
    )


def scores(q_rot, k_rot, allowed):
    raw = jnp.einsum("tkgw,ukw->kgtu", q_rot, k_rot, preferred_element_type=jnp.float32)
    raw = raw * q_rot.shape[-1] ** (-0.5)
    return jnp.where(allowed[None, None], raw, -jnp.inf)


def step_back(s_block, lse, q_rot, k_rot, v_blk, attention_gradient, delta):
    scale = q_rot.shape[-1] ** (-0.5)
    p_wide = jnp.exp(s_block - lse[..., None])
    p_narrow = p_wide.astype(jnp.bfloat16)
    d_prob = jnp.einsum(
        "tkgw,ukw->kgtu", attention_gradient, v_blk, preferred_element_type=jnp.float32
    )
    d_score = (p_wide * (d_prob - delta[..., None])).astype(jnp.bfloat16)
    dq_part = (
        jnp.einsum("kgtu,ukw->tkgw", d_score, k_rot, preferred_element_type=jnp.float32) * scale
    )
    dk_part = (
        jnp.einsum("kgtu,tkgw->ukw", d_score, q_rot, preferred_element_type=jnp.float32) * scale
    )
    dv_part = jnp.einsum(
        "kgtu,tkgw->ukw", p_narrow, attention_gradient, preferred_element_type=jnp.float32
    )
    return (dq_part, dk_part, dv_part)


def shards(
    queries,
    keys,
    values,
    output_gradient,
    output_weight,
    adapter_down,
    adapter_up,
    positions,
    block_pair_mask,
):
    rows = queries.shape[0]
    half_rows = rows // 2
    width = HEAD_SIZE
    kv_local = keys.shape[1] // width
    q_local = queries.shape[1] // width
    groups = q_local // kv_local
    cosine, sine = angles(positions, width)
    q_rot = rotate(queries.reshape(rows, q_local, width).astype(jnp.float32), cosine, sine)
    q_rot = q_rot.astype(jnp.bfloat16).reshape(rows, kv_local, groups, width)
    k_rot = rotate(keys.reshape(rows, kv_local, width).astype(jnp.float32), cosine, sine).astype(
        jnp.bfloat16
    )
    v_own = values.reshape(rows, kv_local, width)
    k_prev, v_prev = shifted((k_rot, v_own), "seq", 1)
    modes = block_pair_mask[0]
    own_code = tile_modes(modes[0], half_rows)
    own_allowed = (own_code == 1) | (own_code == 2) & (positions[None, :] <= positions[:, None])
    prev_allowed = tile_modes(modes[1], half_rows) == 1
    s_own = scores(q_rot, k_rot, own_allowed)
    s_prev = scores(q_rot, k_prev, prev_allowed)
    lse = jnp.logaddexp(jax.nn.logsumexp(s_own, -1), jax.nn.logsumexp(s_prev, -1))
    p_own = jnp.exp(s_own - lse[..., None]).astype(jnp.bfloat16)
    p_prev = jnp.exp(s_prev - lse[..., None]).astype(jnp.bfloat16)
    attn4 = jnp.einsum("kgtu,ukw->tkgw", p_own, v_own, preferred_element_type=jnp.float32)
    attn4 = (
        attn4 + jnp.einsum("kgtu,ukw->tkgw", p_prev, v_prev, preferred_element_type=jnp.float32)
    ).astype(jnp.bfloat16)
    attention_output = attn4.reshape(rows, q_local * width)
    adapter_middle = lax.psum(
        jnp.dot(attention_output, adapter_down, preferred_element_type=jnp.float32), "rep"
    ).astype(jnp.bfloat16)
    backward_result = lax.dot_general(
        output_gradient, adapter_up, (((1,), (1,)), ((), ())), preferred_element_type=jnp.float32
    ).astype(jnp.bfloat16)
    a_term = lax.dot_general(
        backward_result,
        attention_output,
        (((0,), (0,)), ((), ())),
        preferred_element_type=jnp.float32,
    )
    b_term = lax.dot_general(
        adapter_middle,
        lax.dynamic_slice_in_dim(output_gradient, lax.axis_index("rep") * 1024, 1024, 1),
        (((0,), (0,)), ((), ())),
        preferred_element_type=jnp.float32,
    )
    down_gradient, adapter_up_gradient = adapter_sums(a_term, b_term)
    adapter_down_gradient = down_gradient.T
    attention_gradient = lax.dot_general(
        output_gradient, output_weight, (((1,), (1,)), ((), ())), preferred_element_type=jnp.float32
    )
    attention_gradient = attention_gradient + 2.0 * lax.dot_general(
        backward_result, adapter_down, (((1,), (1,)), ((), ())), preferred_element_type=jnp.float32
    )
    d_attn4 = attention_gradient.astype(jnp.bfloat16).reshape(rows, kv_local, groups, width)
    delta = jnp.sum(d_attn4.astype(jnp.float32) * attn4.astype(jnp.float32), -1).transpose(1, 2, 0)
    dq_own, dk_own, dv_own = step_back(s_own, lse, q_rot, k_rot, v_own, d_attn4, delta)
    dq_prev, dk_prev, dv_prev = step_back(s_prev, lse, q_rot, k_prev, v_prev, d_attn4, delta)
    dk_back, dv_back = shifted(
        (dk_prev.astype(jnp.bfloat16), dv_prev.astype(jnp.bfloat16)), "seq", -1
    )
    dq_rot = (dq_own + dq_prev).reshape(rows, q_local, width)
    query_gradient = (
        unrotate(dq_rot, cosine, sine).astype(jnp.bfloat16).reshape(rows, q_local * width)
    )
    key_gradient = (
        unrotate(dk_own + dk_back.astype(jnp.float32), cosine, sine)
        .astype(jnp.bfloat16)
        .reshape(rows, kv_local * width)
    )
    value_gradient = (
        (dv_own + dv_back.astype(jnp.float32)).astype(jnp.bfloat16).reshape(rows, kv_local * width)
    )
    return (
        query_gradient,
        key_gradient,
        value_gradient,
        adapter_down_gradient,
        adapter_up_gradient,
    )


def solution(mesh):
    placed = (
        P("seq", "rep"),
        P("seq", "rep"),
        P("seq", "rep"),
        P("seq", None),
        P("rep", None),
        P("rep", None),
        P(),
        P("seq"),
        P("seq", None, None, None),
    )
    return jax.shard_map(
        shards,
        mesh=mesh,
        in_specs=placed,
        out_specs=(P("seq", "rep"), P("seq", "rep"), P("seq", "rep"), P("rep", None), P()),
        check_vma=False,
    )
```

```python
import jax
import jax.numpy as jnp
from jax import lax
from jax.experimental import pallas as pl
from jax.experimental.pallas import tpu as pltpu
from jax.sharding import PartitionSpec as P

HEAD = 128
ROWS = 512
HALF = 256
HEADS = 8
WIDTH = 4096
MESH = pl.DeviceIdType.MESH
F32 = jnp.float32
BF16 = jnp.bfloat16
SCALE = HEAD**-0.5
LOG2E = 1.4426950408889634
HIDDEN = -1e30

K_NEXT, V_NEXT, MID, RS1A, RS1B, RS2, AG1, AG2, AG3, BACK, COPIES = 0, 1, 2, 6, 14, 22, 30, 38, 46, 50, 52


def dot(a, b):
    return jnp.dot(a, b, preferred_element_type=F32)


def dot_nt(a, b):
    return lax.dot_general(a, b, (((1,), (1,)), ((), ())), preferred_element_type=F32)


def seq_at(j, z):
    return (j // 4) * 32 + z * 4 + j % 4


def layer_kernel(
    q_hbm, k_in, v_in, og_hbm, w_hbm, down_t, up_in, cos_t, sin_t, pos_row, codes,
    dq_out, dk_out, dv_out, a_out, b_out,
    q_nat, og, w, k_all, v_all, k_t, v_t, q_t, diag, weights, attn_t, d_attn_t, back_t, down,
    dk_acc, dv_acc, mid_own, mid_all, back_send, back_recv,
    part_a, part_b, rs1a, rs1b, red1, rs2, ag1, full, b_all,
    load_sem, send_sem, recv_sem,
):
    s, r = lax.axis_index("seq"), lax.axis_index("rep")
    z, j = (s // 4) % 8, (s // 32) * 4 + s % 4
    along_z = [(seq_at(j, (z + o) % 8), r) for o in range(8)]
    along_j = [(seq_at((j + o) % 8, z), r) for o in range(8)]
    along_r = [(s, (r + o) % 4) for o in range(4)]
    after, before = ((s + 1) % 64, r), ((s + 63) % 64, r)
    peers = along_z[1:] + along_j[1:] + along_r[1:] + [after, before]

    def remote(at, src, dst, device):
        return pltpu.make_async_remote_copy(
            src_ref=src, dst_ref=dst, send_sem=send_sem.at[at], recv_sem=recv_sem.at[at],
            device_id=device, device_id_type=MESH,
        )

    def k_next():
        return remote(K_NEXT, k_all.at[:, 0:ROWS], k_all.at[:, ROWS : 2 * ROWS], after)

    def v_next():
        return remote(V_NEXT, v_all.at[:, 0:ROWS], v_all.at[:, ROWS : 2 * ROWS], after)

    def mids():
        return [remote(MID + o, mid_own, mid_all.at[o], along_r[o]) for o in range(1, 4)]

    def rs1_a():
        return [
            remote(RS1A + o, part_a.at[(z + o) % 8], rs1a.at[o], along_z[o]) for o in range(1, 8)
        ]

    def rs1_b():
        return [
            remote(RS1B + o, part_b.at[(z + o) % 8], rs1b.at[o], along_z[o]) for o in range(1, 8)
        ]

    def rs2_all():
        return [remote(RS2 + o, red1.at[(j + o) % 8], rs2.at[o], along_j[o]) for o in range(1, 8)]

    def ag1_all():
        return [remote(AG1 + o, ag1.at[j], ag1.at[j], along_j[o]) for o in range(1, 8)]

    def ag2_all():
        return [remote(AG2 + o, full.at[z], full.at[z], along_z[o]) for o in range(1, 8)]

    def ag3_all():
        return [remote(AG3 + o, b_all.at[r], b_all.at[r], along_r[o]) for o in range(1, 4)]

    def back_copy(g):
        return remote(BACK + g, back_send.at[g], back_recv.at[g], before)

    def begin(copies):
        for copy in copies:
            copy.start()

    def finish(copies):
        for copy in copies:
            copy.wait()

    barrier = pltpu.get_barrier_semaphore()
    for p in peers:
        pl.semaphore_signal(barrier, inc=1, device_id=p, device_id_type=MESH)
    load_q = pltpu.make_async_copy(q_hbm, q_nat, load_sem.at[0])
    load_og = pltpu.make_async_copy(og_hbm, og, load_sem.at[1])
    load_w = pltpu.make_async_copy(w_hbm, w, load_sem.at[2])
    load_q.start()
    load_og.start()
    load_w.start()

    cosine, sine = cos_t[...], sin_t[...]

    def turned(x):
        x1, x2 = x[:64], x[64:]
        return jnp.concatenate([x1 * cosine - x2 * sine, x2 * cosine + x1 * sine], 0)

    for g in range(2):
        v_own = v_in[:, g * HEAD : (g + 1) * HEAD]
        v_all[g, 0:ROWS] = v_own
        v_t[g, :, 0:ROWS] = v_own.astype(F32).T.astype(BF16)
        k_turned = turned(k_in[:, g * HEAD : (g + 1) * HEAD].astype(F32).T)
        k_t[g, :, 0:ROWS] = k_turned.astype(BF16)
        k_all[g, 0:ROWS] = k_turned.T.astype(BF16)
    pl.semaphore_wait(barrier, len(peers))
    k_next().start()
    v_next().start()

    q_pos = pos_row[...]
    k_pos = jnp.broadcast_to(q_pos, (8, ROWS)).T[:, 0:1]

    def hidden(step, a, b):
        return jnp.where(codes[step * 4 + a * 2 + b] == 1, 0.0, HIDDEN).astype(F32)

    for a in range(2):
        code = codes[a * 3]
        early = k_pos[a * HALF : (a + 1) * HALF] <= q_pos[:, a * HALF : (a + 1) * HALF]
        shown = jnp.where(early, jnp.where(code >= 1, 0.0, HIDDEN), jnp.where(code == 1, 0.0, HIDDEN))
        diag[a] = shown.astype(F32)

    down[...] = down_t[...].astype(F32).T.astype(BF16)
    dk_acc[...] = jnp.zeros_like(dk_acc)
    dv_acc[...] = jnp.zeros_like(dv_acc)

    load_q.wait()

    def turn_queries(h, carry):
        x = q_nat[:, pl.ds(pl.multiple_of(h * HEAD, HEAD), HEAD)].astype(F32).T
        q_t[h] = turned(x).astype(BF16)
        return carry

    lax.fori_loop(0, HEADS, turn_queries, 0)

    load_og.wait()
    back_t[...] = dot_nt(up_in[...], og[...]).astype(BF16)

    k_next().wait()
    v_next().wait()
    for g in range(2):
        k_t[g, :, ROWS : 2 * ROWS] = k_all[g, ROWS : 2 * ROWS].astype(F32).T.astype(BF16)
        v_t[g, :, ROWS : 2 * ROWS] = v_all[g, ROWS : 2 * ROWS].astype(F32).T.astype(BF16)

    def forward(h, carry):
        g = h // 4
        for a in range(2):
            cols = slice(a * HALF, (a + 1) * HALF)
            raw = dot(k_all[g], q_t[h, :, cols])
            blocks = []
            for i in range(4):
                block = raw[i * HALF : (i + 1) * HALF]
                if i == a:
                    block = block + diag[a]
                    blocks.append((block, None, jnp.max(block, 0, keepdims=True)))
                else:
                    off = hidden(i // 2, a, i % 2)
                    blocks.append((block, off, jnp.max(block, 0, keepdims=True) + off))
            top = jnp.maximum(
                jnp.maximum(blocks[0][2], blocks[1][2]), jnp.maximum(blocks[2][2], blocks[3][2])
            )
            shift = top * (-SCALE * LOG2E)
            total = jnp.zeros((1, HALF), F32)
            powers = []
            for block, off, _ in blocks:
                e = jnp.exp2(block * (SCALE * LOG2E) + (shift if off is None else shift + off))
                total = total + jnp.sum(e, 0, keepdims=True)
                powers.append(e)
            share = 1.0 / total
            for i in range(4):
                weights[h, i * HALF : (i + 1) * HALF, cols] = (powers[i] * share).astype(BF16)
            attn_t[h, :, cols] = dot(v_t[g], weights[h, :, cols]).astype(BF16)
        return carry

    lax.fori_loop(0, HEADS, forward, 0)

    mid_part = dot(down_t[...], attn_t[...].reshape(HEADS * HEAD, ROWS))
    mid_own[...] = mid_part.astype(BF16)
    begin(mids())
    for h in range(HEADS):
        part_a[h] = dot_nt(back_t[...], attn_t[h])
    begin(rs1_a())

    load_w.wait()

    def project(i, carry):
        at = pl.multiple_of(i * 512, 512)
        x = dot_nt(w[pl.ds(at, 512)], og[...]) + 2.0 * dot(down[pl.ds(at, 512)], back_t[...])
        d_attn_t[pl.ds(i * 4, 4)] = x.astype(BF16).reshape(4, HEAD, ROWS)
        return carry

    lax.fori_loop(0, 2, project, 0)

    finish(mids())
    mid = mid_part
    for o in range(1, 4):
        mid = mid + mid_all[o].astype(F32)
    b_part = dot(mid.astype(BF16), og[:, pl.ds(pl.multiple_of(r * 1024, 1024), 1024)])
    for c in range(8):
        part_b[c] = b_part[:, c * HEAD : (c + 1) * HEAD]
    begin(rs1_b())

    def finish_keys(g):
        back_copy(g).wait()
        dk = dk_acc[g, 0:ROWS] * SCALE + back_recv[g, 0].astype(F32)
        x = dk.T
        x1, x2 = x[:64], x[64:]
        x = jnp.concatenate([x1 * cosine + x2 * sine, x2 * cosine - x1 * sine], 0)
        dk_out[:, g * HEAD : (g + 1) * HEAD] = x.T.astype(BF16)
        dv = dv_acc[g, 0:ROWS] + back_recv[g, 1].astype(F32)
        dv_out[:, g * HEAD : (g + 1) * HEAD] = dv.astype(BF16)

    def send_back(g):
        back_send[g, 0] = (dk_acc[g, ROWS : 2 * ROWS] * SCALE).astype(BF16)
        back_send[g, 1] = dv_acc[g, ROWS : 2 * ROWS].astype(BF16)
        back_copy(g).start()

    def backward(h, carry):
        g = h // 4

        @pl.when(h == 2)
        def _():
            finish(rs1_a())
            finish(rs1_b())
            total_a, total_b = part_a[z], part_b[z]
            for o in range(1, 8):
                total_a = total_a + rs1a[o]
                total_b = total_b + rs1b[o]
            red1[0:4] = total_a.reshape(4, 8, HEAD)
            red1[4:8] = total_b.reshape(4, 8, HEAD)
            begin(rs2_all())

        @pl.when(h == 4)
        def _():
            send_back(0)
            finish(rs2_all())
            total = red1[j]
            for o in range(1, 8):
                total = total + rs2[o]
            ag1[j] = 2.0 * total
            begin(ag1_all())

        @pl.when(h == 6)
        def _():
            finish(ag1_all())
            full[z] = ag1[...].reshape(64, HEAD)
            begin(ag2_all())

        for a in range(2):
            cols = slice(a * HALF, (a + 1) * HALF)
            grad = d_attn_t[h, :, cols]
            delta = jnp.sum(grad.astype(F32) * attn_t[h, :, cols].astype(F32), 0, keepdims=True)
            p = weights[h, :, cols]
            d_score = (p.astype(F32) * (dot(v_all[g], grad) - delta)).astype(BF16)
            dq = dot(k_t[g], d_score) * SCALE
            x1, x2 = dq[:64], dq[64:]
            c, n = cosine[:, cols], sine[:, cols]
            x = jnp.concatenate([x1 * c + x2 * n, x2 * c - x1 * n], 0)
            dq_out[cols, pl.ds(pl.multiple_of(h * HEAD, HEAD), HEAD)] = x.T.astype(BF16)
            dk_acc[g] += dot_nt(d_score, q_t[h, :, cols])
            dv_acc[g] += dot_nt(p, grad)
        return carry

    lax.fori_loop(0, HEADS, backward, 0)
    send_back(1)

    finish(ag2_all())
    b_all[r] = full[:, 32:64, :]
    begin(ag3_all())
    finish_keys(0)
    for c in range(8):
        a_out[:, c * HEAD : (c + 1) * HEAD] = full[c, 0:32, :]
    finish_keys(1)
    finish(ag3_all())
    for p in range(4):
        for c in range(8):
            at = p * 1024 + c * HEAD
            b_out[:, at : at + HEAD] = b_all[p, c]


def shards(
    queries,
    keys,
    values,
    output_gradient,
    output_weight,
    adapter_down,
    adapter_up,
    positions,
    block_pair_mask,
):
    freq = 1000000.0 ** (-(jnp.arange(HEAD // 2).astype(F32) * 2.0 / HEAD))
    pos = positions.astype(F32)
    phase = freq[:, None] * pos[None, :]
    vmem = pl.BlockSpec(memory_space=pltpu.VMEM)
    smem = pl.BlockSpec(memory_space=pltpu.SMEM)
    hbm = pl.BlockSpec(memory_space=pl.ANY)
    out = jax.ShapeDtypeStruct
    dq, dk, dv, a, b = pl.pallas_call(
        layer_kernel,
        out_shape=(
            out((ROWS, HEADS * HEAD), BF16),
            out((ROWS, 2 * HEAD), BF16),
            out((ROWS, 2 * HEAD), BF16),
            out((32, HEADS * HEAD), F32),
            out((32, WIDTH), F32),
        ),
        in_specs=[hbm, vmem, vmem, hbm, hbm, vmem, vmem, vmem, vmem, vmem, smem],
        out_specs=(vmem,) * 5,
        scratch_shapes=[
            pltpu.VMEM((ROWS, HEADS * HEAD), BF16),
            pltpu.VMEM((ROWS, WIDTH), BF16),
            pltpu.VMEM((HEADS * HEAD, WIDTH), BF16),
            pltpu.VMEM((2, 2 * ROWS, HEAD), BF16),
            pltpu.VMEM((2, 2 * ROWS, HEAD), BF16),
            pltpu.VMEM((2, HEAD, 2 * ROWS), BF16),
            pltpu.VMEM((2, HEAD, 2 * ROWS), BF16),
            pltpu.VMEM((HEADS, HEAD, ROWS), BF16),
            pltpu.VMEM((2, HALF, HALF), F32),
            pltpu.VMEM((HEADS, 2 * ROWS, ROWS), BF16),
            pltpu.VMEM((HEADS, HEAD, ROWS), BF16),
            pltpu.VMEM((HEADS, HEAD, ROWS), BF16),
            pltpu.VMEM((32, ROWS), BF16),
            pltpu.VMEM((HEADS * HEAD, 32), BF16),
            pltpu.VMEM((2, 2 * ROWS, HEAD), F32),
            pltpu.VMEM((2, 2 * ROWS, HEAD), F32),
            pltpu.VMEM((32, ROWS), BF16),
            pltpu.VMEM((4, 32, ROWS), BF16),
            pltpu.VMEM((2, 2, ROWS, HEAD), BF16),
            pltpu.VMEM((2, 2, ROWS, HEAD), BF16),
            pltpu.VMEM((8, 32, HEAD), F32),
            pltpu.VMEM((8, 32, HEAD), F32),
            pltpu.VMEM((8, 32, HEAD), F32),
            pltpu.VMEM((8, 32, HEAD), F32),
            pltpu.VMEM((8, 8, HEAD), F32),
            pltpu.VMEM((8, 8, HEAD), F32),
            pltpu.VMEM((8, 8, HEAD), F32),
            pltpu.VMEM((8, 64, HEAD), F32),
            pltpu.VMEM((4, 8, 32, HEAD), F32),
            pltpu.SemaphoreType.DMA((3,)),
            pltpu.SemaphoreType.DMA((COPIES,)),
            pltpu.SemaphoreType.DMA((COPIES,)),
        ],
        compiler_params=pltpu.CompilerParams(
            collective_id=0, has_side_effects=True, vmem_limit_bytes=56 * 1024 * 1024
        ),
    )(
        queries,
        keys,
        values,
        output_gradient,
        output_weight,
        adapter_down.T,
        adapter_up,
        jnp.cos(phase),
        jnp.sin(phase),
        pos[None, :],
        block_pair_mask.reshape(8),
    )
    return dq, dk, dv, a.T, b


def solution(mesh):
    placed = (
        P("seq", "rep"),
        P("seq", "rep"),
        P("seq", "rep"),
        P("seq", None),
        P("rep", None),
        P("rep", None),
        P(),
        P("seq"),
        P("seq", None, None, None),
    )
    return jax.shard_map(
        shards,
        mesh=mesh,
        in_specs=placed,
        out_specs=(P("seq", "rep"), P("seq", "rep"), P("seq", "rep"), P("rep", None), P()),
        check_vma=False,
    )
```

```python
import jax
import jax.numpy as jnp
from jax import lax
from jax.experimental import pallas as pl
from jax.experimental.pallas import tpu as pltpu
from jax.sharding import PartitionSpec as P

HEAD = 128
ROWS = 512
HALF = 256
HEADS = 8
WIDTH = 4096
MESH = pl.DeviceIdType.MESH
F32 = jnp.float32
BF16 = jnp.bfloat16
SCALE = HEAD**-0.5
POWER = SCALE * 1.4426950408889634
HIDDEN = -1e30

K_NEXT, V_NEXT, MID, RS1A, RS1B, ALLJ, AG2, BACK, AG3, COPIES = 0, 2, 4, 8, 16, 24, 32, 40, 42, 74


def dot(a, b):
    return jnp.dot(a, b, preferred_element_type=F32)


def dot_nt(a, b):
    return lax.dot_general(a, b, (((1,), (1,)), ((), ())), preferred_element_type=F32)


def seq_at(j, z):
    return (j // 4) * 32 + z * 4 + j % 4


def layer_kernel(
    q_hbm, k_in, v_in, og_hbm, w_hbm, down_t, up_in, cos_t, sin_t, pos_row, codes,
    dq_out, dk_out, dv_out, a_out, b_out,
    q_nat, og, w, k_all, v_all, k_t, v_t, q_t, diag, weights, stats, attn_own, attn_t, d_attn_t, back_t, down,
    dk_acc, dv_acc, mid_own, mid_all, back_send, back_recv,
    part_a, part_b, rs1a, rs1b, all_j, full, b_all,
    load_sem, send_sem, recv_sem,
):
    s, r = lax.axis_index("seq"), lax.axis_index("rep")
    z, j = (s // 4) % 8, (s // 32) * 4 + s % 4
    along_z = [(seq_at(j, (z + o) % 8), r) for o in range(8)]
    along_j = [(seq_at((j + o) % 8, z), r) for o in range(8)]
    along_r = [(s, (r + o) % 4) for o in range(4)]
    after, before = ((s + 1) % 64, r), ((s + 63) % 64, r)
    peers = along_z[1:] + along_j[1:] + along_r[1:] + [after, before]

    def remote(at, src, dst, device):
        return pltpu.make_async_remote_copy(
            src_ref=src, dst_ref=dst, send_sem=send_sem.at[at], recv_sem=recv_sem.at[at],
            device_id=device, device_id_type=MESH,
        )

    def next_copies(g):
        return [
            remote(K_NEXT + g, k_all.at[g, 0:ROWS], k_all.at[g, ROWS : 2 * ROWS], after),
            remote(V_NEXT + g, v_all.at[g, 0:ROWS], v_all.at[g, ROWS : 2 * ROWS], after),
        ]

    def mids():
        return [remote(MID + o, mid_own, mid_all.at[o], along_r[o]) for o in range(1, 4)]

    def rs1_a():
        return [
            remote(RS1A + o, part_a.at[(z + o) % 8], rs1a.at[o], along_z[o]) for o in range(1, 8)
        ]

    def rs1_b():
        return [
            remote(RS1B + o, part_b.at[(z + o) % 8], rs1b.at[o], along_z[o]) for o in range(1, 8)
        ]

    def all_j_copies():
        return [remote(ALLJ + o, all_j.at[j], all_j.at[j], along_j[o]) for o in range(1, 8)]

    def ag2(o):
        return remote(AG2 + o, full.at[z], full.at[z], along_z[o])

    def ag3(k):
        block = full.at[(z + 8 - k) % 8, 32:64]
        land = b_all.at[r, (z + 8 - k) % 8]
        return [remote(AG3 + k * 4 + o, block, land, along_r[o]) for o in range(1, 4)]

    def back_copy(g):
        return remote(BACK + g, back_send.at[g], back_recv.at[g], before)

    def begin(copies):
        for copy in copies:
            copy.start()

    def finish(copies):
        for copy in copies:
            copy.wait()

    barrier = pltpu.get_barrier_semaphore()
    for p in peers:
        pl.semaphore_signal(barrier, inc=1, device_id=p, device_id_type=MESH)
    load_q = pltpu.make_async_copy(q_hbm, q_nat, load_sem.at[0])
    load_og = pltpu.make_async_copy(og_hbm, og, load_sem.at[1])
    load_w = pltpu.make_async_copy(w_hbm, w, load_sem.at[2])
    load_q.start()
    load_og.start()
    load_w.start()

    cosine, sine = cos_t[...], sin_t[...]

    def turned(x):
        x1, x2 = x[:64], x[64:]
        return jnp.concatenate([x1 * cosine - x2 * sine, x2 * cosine + x1 * sine], 0)

    for g in range(2):
        v_own = v_in[:, g * HEAD : (g + 1) * HEAD]
        v_all[g, 0:ROWS] = v_own
        v_t[g, :, 0:ROWS] = v_own.astype(F32).T.astype(BF16)
        k_turned = turned(k_in[:, g * HEAD : (g + 1) * HEAD].astype(F32).T)
        k_t[g, :, 0:ROWS] = k_turned.astype(BF16)
        k_all[g, 0:ROWS] = k_turned.T.astype(BF16)

    q_pos = pos_row[...].astype(F32)
    k_pos = jnp.broadcast_to(q_pos, (8, ROWS)).T[:, 0:1]

    def hidden(step, a, b):
        return jnp.where(codes[0, step, a, b] == 1, 0.0, HIDDEN).astype(F32)

    for a in range(2):
        code = codes[0, 0, a, a]
        early = k_pos[a * HALF : (a + 1) * HALF] <= q_pos[:, a * HALF : (a + 1) * HALF]
        shown = jnp.where(early, jnp.where(code >= 1, 0.0, HIDDEN), jnp.where(code == 1, 0.0, HIDDEN))
        diag[a] = shown.astype(F32)

    down[...] = down_t[...].astype(F32).T.astype(BF16)
    dk_acc[...] = jnp.zeros_like(dk_acc)
    dv_acc[...] = jnp.zeros_like(dv_acc)

    load_q.wait()

    def turn_queries(h, carry):
        x = q_nat[:, pl.ds(pl.multiple_of(h * HEAD, HEAD), HEAD)].astype(F32).T
        q_t[h] = turned(x).astype(BF16)
        return carry

    lax.fori_loop(0, HEADS, turn_queries, 0)

    pl.semaphore_wait(barrier, len(peers))
    begin(next_copies(0))

    def forward_own(h, carry):
        g = h // 4

        @pl.when(h == 4)
        def _():
            for copy in next_copies(0):
                copy.wait_send()
            begin(next_copies(1))

        for a in range(2):
            cols = slice(a * HALF, (a + 1) * HALF)
            raw = dot(k_all[g, 0:ROWS], q_t[h, :, cols])
            same = raw[a * HALF : (a + 1) * HALF] + diag[a]
            other = raw[(1 - a) * HALF : (2 - a) * HALF]
            off = hidden(0, a, 1 - a)
            top = jnp.maximum(
                jnp.max(same, 0, keepdims=True), jnp.max(other, 0, keepdims=True) + off
            )
            shift = top * -POWER
            same = jnp.exp2(same * POWER + shift)
            other = jnp.exp2(other * POWER + (shift + off))
            weights[h, a * HALF : (a + 1) * HALF, cols] = same.astype(BF16)
            weights[h, (1 - a) * HALF : (2 - a) * HALF, cols] = other.astype(BF16)
            stats[h, 0:1, cols] = top
            stats[h, 1:2, cols] = jnp.sum(same, 0, keepdims=True) + jnp.sum(other, 0, keepdims=True)
            attn_own[h, :, cols] = dot(v_t[g, :, 0:ROWS], weights[h, 0:ROWS, cols])
        return carry

    lax.fori_loop(0, HEADS, forward_own, 0)

    def take_previous(g):
        for copy in next_copies(g):
            copy.wait_recv()
        k_t[g, :, ROWS : 2 * ROWS] = k_all[g, ROWS : 2 * ROWS].astype(F32).T.astype(BF16)
        v_t[g, :, ROWS : 2 * ROWS] = v_all[g, ROWS : 2 * ROWS].astype(F32).T.astype(BF16)

    def forward_previous(h, carry):
        g = h // 4

        @pl.when(h == 0)
        def _():
            take_previous(0)

        @pl.when(h == 4)
        def _():
            load_og.wait()
            back_t[...] = dot_nt(up_in[...], og[...]).astype(BF16)
            for copy in next_copies(1):
                copy.wait_send()
            take_previous(1)

        for a in range(2):
            cols = slice(a * HALF, (a + 1) * HALF)
            raw = dot(k_all[g, ROWS : 2 * ROWS], q_t[h, :, cols])
            first, second = raw[0:HALF], raw[HALF:ROWS]
            off1, off2 = hidden(1, a, 0), hidden(1, a, 1)
            top = jnp.maximum(
                jnp.max(first, 0, keepdims=True) + off1, jnp.max(second, 0, keepdims=True) + off2
            )
            shift = jnp.minimum(top * -POWER, 1e28)
            first = jnp.exp2(first * POWER + (shift + off1))
            second = jnp.exp2(second * POWER + (shift + off2))
            weights[h, ROWS : ROWS + HALF, cols] = first.astype(BF16)
            weights[h, ROWS + HALF : 2 * ROWS, cols] = second.astype(BF16)
            total = jnp.sum(first, 0, keepdims=True) + jnp.sum(second, 0, keepdims=True)
            top_own = stats[h, 0:1, cols]
            top_all = jnp.maximum(top, top_own)
            own = jnp.exp2((top_own - top_all) * POWER)
            previous = jnp.exp2((top - top_all) * POWER)
            share = 1.0 / (stats[h, 1:2, cols] * own + total * previous)
            own, previous = own * share, previous * share
            stats[h, 2:3, cols] = own
            stats[h, 3:4, cols] = previous
            part = dot(v_t[g, :, ROWS : 2 * ROWS], weights[h, ROWS : 2 * ROWS, cols])
            attn_t[h, :, cols] = (attn_own[h, :, cols] * own + part * previous).astype(BF16)
        return carry

    lax.fori_loop(0, HEADS, forward_previous, 0)

    mid_part = dot(down_t[...], attn_t[...].reshape(HEADS * HEAD, ROWS))
    mid_own[...] = mid_part.astype(BF16)
    begin(mids())
    for h in range(HEADS):
        part_a[h] = dot_nt(back_t[...], attn_t[h]).astype(BF16)
    begin(rs1_a())

    load_w.wait()

    def project(i, carry):
        at = pl.multiple_of(i * 512, 512)
        x = dot_nt(w[pl.ds(at, 512)], og[...]) + 2.0 * dot(down[pl.ds(at, 512)], back_t[...])
        d_attn_t[pl.ds(i * 4, 4)] = x.astype(BF16).reshape(4, HEAD, ROWS)
        return carry

    lax.fori_loop(0, 2, project, 0)

    finish(mids())
    mid = mid_part
    for o in range(1, 4):
        mid = mid + mid_all[o].astype(F32)
    b_part = dot(mid.astype(BF16), og[:, pl.ds(pl.multiple_of(r * 1024, 1024), 1024)])
    for c in range(8):
        part_b[c] = b_part[:, c * HEAD : (c + 1) * HEAD].astype(BF16)
    begin(rs1_b())

    def finish_keys(g):
        back_copy(g).wait()
        dk = dk_acc[g, 0:ROWS] * SCALE + back_recv[g, 0].astype(F32)
        x = dk.T
        x1, x2 = x[:64], x[64:]
        x = jnp.concatenate([x1 * cosine + x2 * sine, x2 * cosine - x1 * sine], 0)
        dk_out[:, g * HEAD : (g + 1) * HEAD] = x.T.astype(BF16)
        dv = dv_acc[g, 0:ROWS] + back_recv[g, 1].astype(F32)
        dv_out[:, g * HEAD : (g + 1) * HEAD] = dv.astype(BF16)

    def send_back(g):
        back_send[g, 0] = (dk_acc[g, ROWS : 2 * ROWS] * SCALE).astype(BF16)
        back_send[g, 1] = dv_acc[g, ROWS : 2 * ROWS].astype(BF16)
        back_copy(g).start()

    def backward(h, carry):
        g = h // 4

        @pl.when(h == 2)
        def _():
            finish(rs1_a())
            finish(rs1_b())
            total_a, total_b = part_a[z].astype(F32), part_b[z].astype(F32)
            for o in range(1, 8):
                total_a = total_a + rs1a[o].astype(F32)
                total_b = total_b + rs1b[o].astype(F32)
            all_j[j, 0:32] = total_a
            all_j[j, 32:64] = total_b
            begin(all_j_copies())

        @pl.when(h == 4)
        def _():
            send_back(0)

        @pl.when(h == 5)
        def _():
            finish(all_j_copies())
            total = all_j[0]
            for o in range(1, 8):
                total = total + all_j[o]
            full[z] = (2.0 * total).astype(BF16)
            begin([ag2(o) for o in range(1, 8)])
            begin(ag3(0))

        @pl.when(h == 7)
        def _():
            for o in range(1, 8):
                ag2(o).wait()
                begin(ag3(o))

        for a in range(2):
            cols = slice(a * HALF, (a + 1) * HALF)
            grad = d_attn_t[h, :, cols]
            delta = jnp.sum(grad.astype(F32) * attn_t[h, :, cols].astype(F32), 0, keepdims=True)
            d_weight = dot(v_all[g], grad)
            q_cols = q_t[h, :, cols]
            dq = None
            for t in range(2):
                rows = slice(t * ROWS, (t + 1) * ROWS)
                factor = stats[h, 2 + t : 3 + t, cols]
                p = weights[h, rows, cols]
                d_score = p.astype(F32) * (d_weight[rows] * factor - delta * factor)
                d_score = d_score.astype(BF16)
                part = dot(k_t[g, :, rows], d_score)
                dq = part if dq is None else dq + part
                dk_acc[g, rows] += dot_nt(d_score, q_cols)
                dv_acc[g, rows] += dot_nt(p, (grad.astype(F32) * factor).astype(BF16))
            dq = dq * SCALE
            x1, x2 = dq[:64], dq[64:]
            c, n = cosine[:, cols], sine[:, cols]
            x = jnp.concatenate([x1 * c + x2 * n, x2 * c - x1 * n], 0)
            dq_out[cols, pl.ds(pl.multiple_of(h * HEAD, HEAD), HEAD)] = x.T.astype(BF16)
        return carry

    lax.fori_loop(0, HEADS, backward, 0)
    send_back(1)
    finish_keys(0)
    b_all[r] = full[:, 32:64, :]
    for c in range(8):
        a_out[:, c * HEAD : (c + 1) * HEAD] = full[c, 0:32].astype(F32)
    finish_keys(1)
    for k in range(8):
        finish(ag3(k))
    b_out[...] = b_all[...]


def write_kernel(
    dq, dk, dv, a, b, dq_out, dk_out, dv_out, a_out, b_out,
    dq_in, dk_in, dv_in, a_in, b_in, b_wide, in_sem, out_sem,
):
    quarter = ROWS // 4
    steps = [(dk, dk_in, dk_out), (dv, dv_in, dv_out), (a, a_in, a_out)]
    for i in range(4):
        rows = slice(i * quarter, (i + 1) * quarter)
        steps.append((dq.at[rows], dq_in.at[rows], dq_out.at[rows]))
    loads = [pltpu.make_async_copy(x, y, in_sem.at[i]) for i, (x, y, _) in enumerate(steps)]
    stores = [pltpu.make_async_copy(y, o, out_sem.at[i]) for i, (_, y, o) in enumerate(steps)]
    load_b = pltpu.make_async_copy(b, b_in, in_sem.at[7])
    store_b = pltpu.make_async_copy(b_wide, b_out, out_sem.at[7])
    load_b.start()
    for copy in loads:
        copy.start()
    load_b.wait()
    for p in range(4):
        for c in range(8):
            at = p * 1024 + c * HEAD
            b_wide[:, at : at + HEAD] = b_in[p, c].astype(F32)
    store_b.start()
    for load, store in zip(loads, stores):
        load.wait()
        store.start()
    for copy in stores:
        copy.wait()
    store_b.wait()


def shards(
    queries,
    keys,
    values,
    output_gradient,
    output_weight,
    adapter_down,
    adapter_up,
    positions,
    block_pair_mask,
):
    freq = 1000000.0 ** (-(jnp.arange(HEAD // 2).astype(F32) * 2.0 / HEAD))
    phase = freq[:, None] * positions.astype(F32)[None, :]
    vmem = pl.BlockSpec(memory_space=pltpu.VMEM)
    smem = pl.BlockSpec(memory_space=pltpu.SMEM)
    hbm = pl.BlockSpec(memory_space=pl.ANY)
    out = jax.ShapeDtypeStruct
    dq, dk, dv, a, b = pl.pallas_call(
        layer_kernel,
        out_shape=(
            out((ROWS, HEADS * HEAD), BF16),
            out((ROWS, 2 * HEAD), BF16),
            out((ROWS, 2 * HEAD), BF16),
            out((32, HEADS * HEAD), F32),
            out((4, 8, 32, HEAD), BF16),
        ),
        in_specs=[hbm, vmem, vmem, hbm, hbm, vmem, vmem, vmem, vmem, vmem, smem],
        out_specs=(vmem,) * 5,
        scratch_shapes=[
            pltpu.VMEM((ROWS, HEADS * HEAD), BF16),
            pltpu.VMEM((ROWS, WIDTH), BF16),
            pltpu.VMEM((HEADS * HEAD, WIDTH), BF16),
            pltpu.VMEM((2, 2 * ROWS, HEAD), BF16),
            pltpu.VMEM((2, 2 * ROWS, HEAD), BF16),
            pltpu.VMEM((2, HEAD, 2 * ROWS), BF16),
            pltpu.VMEM((2, HEAD, 2 * ROWS), BF16),
            pltpu.VMEM((HEADS, HEAD, ROWS), BF16),
            pltpu.VMEM((2, HALF, HALF), F32),
            pltpu.VMEM((HEADS, 2 * ROWS, ROWS), BF16),
            pltpu.VMEM((HEADS, 8, ROWS), F32),
            pltpu.VMEM((HEADS, HEAD, ROWS), F32),
            pltpu.VMEM((HEADS, HEAD, ROWS), BF16),
            pltpu.VMEM((HEADS, HEAD, ROWS), BF16),
            pltpu.VMEM((32, ROWS), BF16),
            pltpu.VMEM((HEADS * HEAD, 32), BF16),
            pltpu.VMEM((2, 2 * ROWS, HEAD), F32),
            pltpu.VMEM((2, 2 * ROWS, HEAD), F32),
            pltpu.VMEM((32, ROWS), BF16),
            pltpu.VMEM((4, 32, ROWS), BF16),
            pltpu.VMEM((2, 2, ROWS, HEAD), BF16),
            pltpu.VMEM((2, 2, ROWS, HEAD), BF16),
            pltpu.VMEM((8, 32, HEAD), BF16),
            pltpu.VMEM((8, 32, HEAD), BF16),
            pltpu.VMEM((8, 32, HEAD), BF16),
            pltpu.VMEM((8, 32, HEAD), BF16),
            pltpu.VMEM((8, 64, HEAD), F32),
            pltpu.VMEM((8, 64, HEAD), BF16),
            pltpu.VMEM((4, 8, 32, HEAD), BF16),
            pltpu.SemaphoreType.DMA((3,)),
            pltpu.SemaphoreType.DMA((COPIES,)),
            pltpu.SemaphoreType.DMA((COPIES,)),
        ],
        compiler_params=pltpu.CompilerParams(
            collective_id=0, has_side_effects=True, vmem_limit_bytes=56 * 1024 * 1024
        ),
    )(
        queries,
        keys,
        values,
        output_gradient,
        output_weight,
        adapter_down.T,
        adapter_up,
        jnp.cos(phase),
        jnp.sin(phase),
        positions[None, :],
        block_pair_mask,
    )
    dq, dk, dv, a, b = pl.pallas_call(
        write_kernel,
        out_shape=(
            out((ROWS, HEADS * HEAD), BF16),
            out((ROWS, 2 * HEAD), BF16),
            out((ROWS, 2 * HEAD), BF16),
            out((32, HEADS * HEAD), F32),
            out((32, WIDTH), F32),
        ),
        in_specs=[hbm] * 5,
        out_specs=(hbm,) * 5,
        scratch_shapes=[
            pltpu.VMEM((ROWS, HEADS * HEAD), BF16),
            pltpu.VMEM((ROWS, 2 * HEAD), BF16),
            pltpu.VMEM((ROWS, 2 * HEAD), BF16),
            pltpu.VMEM((32, HEADS * HEAD), F32),
            pltpu.VMEM((4, 8, 32, HEAD), BF16),
            pltpu.VMEM((32, WIDTH), F32),
            pltpu.SemaphoreType.DMA((8,)),
            pltpu.SemaphoreType.DMA((8,)),
        ],
    )(dq, dk, dv, a, b)
    return dq, dk, dv, a.T, b


def solution(mesh):
    placed = (
        P("seq", "rep"),
        P("seq", "rep"),
        P("seq", "rep"),
        P("seq", None),
        P("rep", None),
        P("rep", None),
        P(),
        P("seq"),
        P("seq", None, None, None),
    )
    return jax.shard_map(
        shards,
        mesh=mesh,
        in_specs=placed,
        out_specs=(P("seq", "rep"), P("seq", "rep"), P("seq", "rep"), P("rep", None), P()),
        check_vma=False,
    )
```

```python
import jax
import jax.numpy as jnp
import numpy as np
from jax import lax
from jax.experimental import pallas as pl
from jax.experimental.pallas import tpu as pltpu
from jax.sharding import PartitionSpec as P

HEAD = 128
ROWS = 512
HALF = 256
HEADS = 8
WIDTH = 4096
MESH = pl.DeviceIdType.MESH
F32 = jnp.float32
BF16 = jnp.bfloat16
SCALE = HEAD**-0.5
POWER = SCALE * 1.4426950408889634
HIDDEN = -1e30
AT_ONCE = 4
FREQUENCY = (1000000.0 ** (-np.arange(64) * 2.0 / 128)).astype(np.float32)

K_NEXT, V_NEXT, MID, RS1A, RS1B, ALLJ, AG2, BACK, AG3, COPIES = 0, 2, 4, 8, 16, 24, 32, 40, 42, 74


def dot(a, b):
    return jnp.dot(a, b, preferred_element_type=F32)


def dot_nt(a, b):
    return lax.dot_general(a, b, (((1,), (1,)), ((), ())), preferred_element_type=F32)


def seq_at(j, z):
    return (j // 4) * 32 + z * 4 + j % 4


def layer_kernel(
    q_hbm, k_hbm, v_hbm, og_hbm, w_hbm, down_hbm, up_hbm, freq, pos_row, codes,
    dq_hbm, dk_hbm, dv_hbm, a_hbm, b_out,
    k_nat, up, down_t, angle, dq_out, dk_out, dv_out, a_out,
    q_nat, og, w, k_all, v_all, k_t, v_t, q_t, diag, weights, stats, attn_own, attn_t, d_attn_t, back_t, down,
    dk_acc, dv_acc, mid_own, mid_all, back_send, back_recv,
    part_a, part_b, rs1a, rs1b, all_j, full, b_all,
    load_sem, store_sem, send_sem, recv_sem,
):
    s, r = lax.axis_index("seq"), lax.axis_index("rep")
    z, j = (s // 4) % 8, (s // 32) * 4 + s % 4
    along_z = [(seq_at(j, (z + o) % 8), r) for o in range(8)]
    along_j = [(seq_at((j + o) % 8, z), r) for o in range(8)]
    along_r = [(s, (r + o) % 4) for o in range(4)]
    after, before = ((s + 1) % 64, r), ((s + 63) % 64, r)
    peers = along_z[1:] + along_j[1:] + along_r[1:] + [after, before]

    def remote(at, src, dst, device):
        return pltpu.make_async_remote_copy(
            src_ref=src, dst_ref=dst, send_sem=send_sem.at[at], recv_sem=recv_sem.at[at],
            device_id=device, device_id_type=MESH,
        )

    def next_v(g):
        return remote(V_NEXT + g, v_all.at[g, 0:ROWS], v_all.at[g, ROWS : 2 * ROWS], after)

    def next_k(g):
        return remote(K_NEXT + g, k_all.at[g, 0:ROWS], k_all.at[g, ROWS : 2 * ROWS], after)

    def mids():
        return [remote(MID + o, mid_own, mid_all.at[o], along_r[o]) for o in range(1, 4)]

    def rs1_a():
        return [
            remote(RS1A + o, part_a.at[(z + o) % 8], rs1a.at[o], along_z[o]) for o in range(1, 8)
        ]

    def rs1_b():
        return [
            remote(RS1B + o, part_b.at[(z + o) % 8], rs1b.at[o], along_z[o]) for o in range(1, 8)
        ]

    def all_j_copies():
        return [remote(ALLJ + o, all_j.at[j], all_j.at[j], along_j[o]) for o in range(1, 8)]

    def ag2(o):
        return remote(AG2 + o, full.at[z], full.at[z], along_z[o])

    def ag3(k):
        block = full.at[(z + 8 - k) % 8, 32:64]
        land = b_all.at[r, (z + 8 - k) % 8]
        return [remote(AG3 + k * 4 + o, block, land, along_r[o]) for o in range(1, 4)]

    def back_copy(g):
        return remote(BACK + g, back_send.at[g], back_recv.at[g], before)

    def begin(copies):
        for copy in copies:
            copy.start()

    def finish(copies):
        for copy in copies:
            copy.wait()

    barrier = pltpu.get_barrier_semaphore()
    for p in peers:
        pl.semaphore_signal(barrier, inc=1, device_id=p, device_id_type=MESH)
    loads = []
    for at, (src, dst) in enumerate([
        (v_hbm.at[:, 0:HEAD], v_all.at[0, 0:ROWS]),
        (v_hbm.at[:, HEAD : 2 * HEAD], v_all.at[1, 0:ROWS]),
        (k_hbm, k_nat), (q_hbm, q_nat), (og_hbm, og), (up_hbm, up), (down_hbm, down_t), (w_hbm, w),
    ]):
        loads.append(pltpu.make_async_copy(src, dst, load_sem.at[at]))
        loads[at].start()
    load_v0, load_v1, load_k, load_q, load_og, load_up, load_down, load_w = loads

    load_v0.wait()
    pl.semaphore_wait(barrier, len(peers))
    next_v(0).start()
    q_pos = pos_row[...].astype(F32)
    phase = freq[:, 0:1] * q_pos
    angle[0] = jnp.cos(phase)
    angle[1] = jnp.sin(phase)
    cosine, sine = angle[0], angle[1]

    def turned(x):
        x1, x2 = x[:64], x[64:]
        return jnp.concatenate([x1 * cosine - x2 * sine, x2 * cosine + x1 * sine], 0)

    load_k.wait()
    for g in range(2):
        k_turned = turned(k_nat[:, g * HEAD : (g + 1) * HEAD].astype(F32).T)
        k_t[g, :, 0:ROWS] = k_turned.astype(BF16)
        k_all[g, 0:ROWS] = k_turned.T.astype(BF16)
        if g == 0:
            next_k(0).start()
    load_v1.wait()
    for g in range(2):
        v_t[g, :, 0:ROWS] = v_all[g, 0:ROWS].astype(F32).T.astype(BF16)

    k_pos = jnp.broadcast_to(q_pos, (8, ROWS)).T[:, 0:1]

    def hidden(step, a, b):
        return jnp.where(codes[0, step, a, b] == 1, 0.0, HIDDEN).astype(F32)

    for a in range(2):
        code = codes[0, 0, a, a]
        early = k_pos[a * HALF : (a + 1) * HALF] <= q_pos[:, a * HALF : (a + 1) * HALF]
        shown = jnp.where(early, jnp.where(code >= 1, 0.0, HIDDEN), jnp.where(code == 1, 0.0, HIDDEN))
        diag[a] = shown.astype(F32)

    load_q.wait()

    def turn_queries(h, carry):
        x = q_nat[:, pl.ds(pl.multiple_of(h * HEAD, HEAD), HEAD)].astype(F32).T
        q_t[h] = turned(x).astype(BF16)
        return carry

    lax.fori_loop(0, HEADS, turn_queries, 0)

    def forward_own(i, carry):
        heads = [i * AT_ONCE + u for u in range(AT_ONCE)]
        g = heads[0] // 4

        raws = [dot(k_all[g, 0:ROWS], q_t[h]) for h in heads]
        rounded = []
        for h, raw in zip(heads, raws):
            columns = []
            for a in range(2):
                cols = slice(a * HALF, (a + 1) * HALF)
                same = raw[cols, cols] + diag[a]
                other = raw[(1 - a) * HALF : (2 - a) * HALF, cols]
                off = hidden(0, a, 1 - a)
                top = jnp.maximum(
                    jnp.max(same, 0, keepdims=True), jnp.max(other, 0, keepdims=True) + off
                )
                shift = top * -POWER
                same = jnp.exp2(same * POWER + shift)
                other = jnp.exp2(other * POWER + (shift + off))
                total = jnp.sum(same, 0, keepdims=True) + jnp.sum(other, 0, keepdims=True)
                stats[h, 0:1, cols] = top
                stats[h, 1:2, cols] = total
                pair = [same, other] if a == 0 else [other, same]
                columns.append(jnp.concatenate(pair, 0).astype(BF16))
            rounded.append(jnp.concatenate(columns, 1))
        for h, e in zip(heads, rounded):
            weights[h, 0:ROWS] = e
            attn_own[h] = dot(v_t[g, :, 0:ROWS], e)
        return carry

    lax.fori_loop(0, HEADS // AT_ONCE, forward_own, 0)

    next_v(0).wait_send()
    next_k(0).wait_send()
    next_v(1).start()
    next_k(1).start()
    load_og.wait()
    load_up.wait()
    load_down.wait()
    back_t[...] = dot_nt(up[...], og[...]).astype(BF16)
    down[...] = down_t[...].astype(F32).T.astype(BF16)
    load_w.wait()

    def project(i, carry):
        at = pl.multiple_of(i * 512, 512)
        x = dot_nt(w[pl.ds(at, 512)], og[...]) + 2.0 * dot(down[pl.ds(at, 512)], back_t[...])
        d_attn_t[pl.ds(i * 4, 4)] = x.astype(BF16).reshape(4, HEAD, ROWS)
        return carry

    lax.fori_loop(0, 2, project, 0)

    def take_previous(g):
        next_v(g).wait_recv()
        next_k(g).wait_recv()
        k_t[g, :, ROWS : 2 * ROWS] = k_all[g, ROWS : 2 * ROWS].astype(F32).T.astype(BF16)
        v_t[g, :, ROWS : 2 * ROWS] = v_all[g, ROWS : 2 * ROWS].astype(F32).T.astype(BF16)

    def forward_previous(i, carry):
        heads = [i * AT_ONCE + u for u in range(AT_ONCE)]
        g = heads[0] // 4

        @pl.when(heads[0] == 0)
        def _():
            take_previous(0)

        @pl.when(heads[0] == 4)
        def _():
            next_v(1).wait_send()
            next_k(1).wait_send()
            take_previous(1)

        raws = [dot(k_all[g, ROWS : 2 * ROWS], q_t[h]) for h in heads]
        rounded, factors = [], []
        for h, raw in zip(heads, raws):
            columns, pairs = [], []
            for a in range(2):
                cols = slice(a * HALF, (a + 1) * HALF)
                first, second = raw[0:HALF, cols], raw[HALF:ROWS, cols]
                off1, off2 = hidden(1, a, 0), hidden(1, a, 1)
                top = jnp.maximum(
                    jnp.max(first, 0, keepdims=True) + off1, jnp.max(second, 0, keepdims=True) + off2
                )
                shift = jnp.minimum(top * -POWER, 1e28)
                first = jnp.exp2(first * POWER + (shift + off1))
                second = jnp.exp2(second * POWER + (shift + off2))
                total = jnp.sum(first, 0, keepdims=True) + jnp.sum(second, 0, keepdims=True)
                top_own = stats[h, 0:1, cols]
                top_all = jnp.maximum(top, top_own)
                own = jnp.exp2((top_own - top_all) * POWER)
                previous = jnp.exp2((top - top_all) * POWER)
                share = 1.0 / (stats[h, 1:2, cols] * own + total * previous)
                own, previous = own * share, previous * share
                stats[h, 2:3, cols] = own
                stats[h, 3:4, cols] = previous
                columns.append(jnp.concatenate([first, second], 0).astype(BF16))
                pairs.append((own, previous))
            rounded.append(jnp.concatenate(columns, 1))
            factors.append([jnp.concatenate(x, 1) for x in zip(*pairs)])
        for h, e, (own, previous) in zip(heads, rounded, factors):
            weights[h, ROWS : 2 * ROWS] = e
            part = dot(v_t[g, :, ROWS : 2 * ROWS], e)
            attn_t[h] = (attn_own[h] * own + part * previous).astype(BF16)
        return carry

    lax.fori_loop(0, HEADS // AT_ONCE, forward_previous, 0)

    mid_part = dot(down_t[...], attn_t[...].reshape(HEADS * HEAD, ROWS))
    mid_own[...] = mid_part.astype(BF16)
    begin(mids())
    for h in range(HEADS):
        part_a[h] = dot_nt(back_t[...], attn_t[h]).astype(BF16)
    begin(rs1_a())

    def backward(t, g):
        rows = slice(t * ROWS, (t + 1) * ROWS)
        heads = range(g * 4, g * 4 + 4)
        d_weights = [dot(v_all[g, rows], d_attn_t[h]) for h in heads]
        d_scores, scaled = [], []
        for h, d_weight in zip(heads, d_weights):
            grad = d_attn_t[h].astype(F32)
            factor = stats[h, 2 + t : 3 + t]
            if t == 1:
                stats[h, 4:5] = jnp.sum(grad * attn_t[h].astype(F32), 0, keepdims=True)
            delta = stats[h, 4:5]
            p = weights[h, rows].astype(F32)
            d_scores.append((p * (d_weight * factor - delta * factor)).astype(BF16))
            scaled.append((grad * factor).astype(BF16))
        dk = [dot_nt(x, q_t[h]) for h, x in zip(heads, d_scores)]
        dv = [dot_nt(weights[h, rows], x) for h, x in zip(heads, scaled)]
        dk, dv = sum(dk[1:], dk[0]) * SCALE, sum(dv[1:], dv[0])
        if t == 1:
            back_send[g, 0] = dk.astype(BF16)
            back_send[g, 1] = dv.astype(BF16)
            back_copy(g).start()
        else:
            dk_acc[g] = dk
            dv_acc[g] = dv
        for h, x in zip(heads, d_scores):
            dq = dot(k_t[g, :, rows], x)
            if t == 1:
                attn_own[h] = dq
            else:
                dq = (dq + attn_own[h]) * SCALE
                x1, x2 = dq[:64], dq[64:]
                dq = jnp.concatenate([x1 * cosine + x2 * sine, x2 * cosine - x1 * sine], 0)
                dq_out[:, h * HEAD : (h + 1) * HEAD] = dq.T.astype(BF16)

    def finish_keys(g):
        back_copy(g).wait()
        x = (dk_acc[g] + back_recv[g, 0].astype(F32)).T
        x1, x2 = x[:64], x[64:]
        x = jnp.concatenate([x1 * cosine + x2 * sine, x2 * cosine - x1 * sine], 0)
        dk_out[:, g * HEAD : (g + 1) * HEAD] = x.T.astype(BF16)
        dv = dv_acc[g] + back_recv[g, 1].astype(F32)
        dv_out[:, g * HEAD : (g + 1) * HEAD] = dv.astype(BF16)

    stores = [
        pltpu.make_async_copy(src, dst, store_sem.at[i])
        for i, (src, dst) in enumerate([
            (dq_out.at[:, 0:512], dq_hbm.at[:, 0:512]),
            (dq_out.at[:, 512:1024], dq_hbm.at[:, 512:1024]),
            (dk_out, dk_hbm), (dv_out, dv_hbm), (a_out, a_hbm),
        ])
    ]

    backward(1, 0)
    finish(mids())
    mid = mid_part
    for o in range(1, 4):
        mid = mid + mid_all[o].astype(F32)
    b_part = dot(mid.astype(BF16), og[:, pl.ds(pl.multiple_of(r * 1024, 1024), 1024)])
    for c in range(8):
        part_b[c] = b_part[:, c * HEAD : (c + 1) * HEAD].astype(BF16)
    begin(rs1_b())

    backward(1, 1)
    finish(rs1_a())
    finish(rs1_b())
    total_a, total_b = part_a[z].astype(F32), part_b[z].astype(F32)
    for o in range(1, 8):
        total_a = total_a + rs1a[o].astype(F32)
        total_b = total_b + rs1b[o].astype(F32)
    all_j[j, 0:32] = total_a.astype(BF16)
    all_j[j, 32:64] = total_b.astype(BF16)
    begin(all_j_copies())

    backward(0, 0)
    stores[0].start()
    finish(all_j_copies())
    total = all_j[0].astype(F32)
    for o in range(1, 8):
        total = total + all_j[o].astype(F32)
    full[z] = (2.0 * total).astype(BF16)
    begin([ag2(o) for o in range(1, 8)])
    begin(ag3(0))

    backward(0, 1)
    stores[1].start()
    for o in range(1, 8):
        ag2(o).wait()
        begin(ag3(o))
    b_all[r] = full[:, 32:64, :]
    for c in range(8):
        a_out[:, c * HEAD : (c + 1) * HEAD] = full[c, 0:32].astype(F32)
    stores[4].start()
    finish_keys(0)
    finish_keys(1)
    stores[2].start()
    stores[3].start()
    for k in range(8):
        finish(ag3(k))
    b_out[...] = b_all[...]
    finish(stores)


def write_kernel(
    dq, dk, dv, a, b, dq_out, dk_out, dv_out, a_out, b_out,
    dq_in, dk_in, dv_in, a_in, b_in, b_wide, in_sem, out_sem,
):
    quarter = ROWS // 4
    steps = [(dk, dk_in, dk_out), (dv, dv_in, dv_out), (a, a_in, a_out)]
    for i in range(4):
        rows = slice(i * quarter, (i + 1) * quarter)
        steps.append((dq.at[rows], dq_in.at[rows], dq_out.at[rows]))
    loads = [pltpu.make_async_copy(x, y, in_sem.at[i]) for i, (x, y, _) in enumerate(steps)]
    stores = [pltpu.make_async_copy(y, o, out_sem.at[i]) for i, (_, y, o) in enumerate(steps)]
    load_b = pltpu.make_async_copy(b, b_in, in_sem.at[7])
    store_b = pltpu.make_async_copy(b_wide, b_out, out_sem.at[7])
    load_b.start()
    for copy in loads:
        copy.start()
    load_b.wait()
    for p in range(4):
        for c in range(8):
            at = p * 1024 + c * HEAD
            b_wide[:, at : at + HEAD] = b_in[p, c].astype(F32)
    store_b.start()
    for load, store in zip(loads, stores):
        load.wait()
        store.start()
    for copy in stores:
        copy.wait()
    store_b.wait()


def shards(
    queries,
    keys,
    values,
    output_gradient,
    output_weight,
    adapter_down,
    adapter_up,
    positions,
    block_pair_mask,
):
    vmem = pl.BlockSpec(memory_space=pltpu.VMEM)
    smem = pl.BlockSpec(memory_space=pltpu.SMEM)
    hbm = pl.BlockSpec(memory_space=pl.ANY)
    out = jax.ShapeDtypeStruct
    dq, dk, dv, a, b = pl.pallas_call(
        layer_kernel,
        out_shape=(
            out((ROWS, HEADS * HEAD), BF16),
            out((ROWS, 2 * HEAD), BF16),
            out((ROWS, 2 * HEAD), BF16),
            out((32, HEADS * HEAD), F32),
            out((4, 8, 32, HEAD), BF16),
        ),
        in_specs=[hbm] * 7 + [vmem, vmem, smem],
        out_specs=(hbm,) * 4 + (vmem,),
        scratch_shapes=[
            pltpu.VMEM((ROWS, 2 * HEAD), BF16),
            pltpu.VMEM((32, WIDTH), BF16),
            pltpu.VMEM((32, HEADS * HEAD), BF16),
            pltpu.VMEM((2, 64, ROWS), F32),
            pltpu.VMEM((ROWS, HEADS * HEAD), BF16),
            pltpu.VMEM((ROWS, 2 * HEAD), BF16),
            pltpu.VMEM((ROWS, 2 * HEAD), BF16),
            pltpu.VMEM((32, HEADS * HEAD), F32),
            pltpu.VMEM((ROWS, HEADS * HEAD), BF16),
            pltpu.VMEM((ROWS, WIDTH), BF16),
            pltpu.VMEM((HEADS * HEAD, WIDTH), BF16),
            pltpu.VMEM((2, 2 * ROWS, HEAD), BF16),
            pltpu.VMEM((2, 2 * ROWS, HEAD), BF16),
            pltpu.VMEM((2, HEAD, 2 * ROWS), BF16),
            pltpu.VMEM((2, HEAD, 2 * ROWS), BF16),
            pltpu.VMEM((HEADS, HEAD, ROWS), BF16),
            pltpu.VMEM((2, HALF, HALF), F32),
            pltpu.VMEM((HEADS, 2 * ROWS, ROWS), BF16),
            pltpu.VMEM((HEADS, 8, ROWS), F32),
            pltpu.VMEM((HEADS, HEAD, ROWS), F32),
            pltpu.VMEM((HEADS, HEAD, ROWS), BF16),
            pltpu.VMEM((HEADS, HEAD, ROWS), BF16),
            pltpu.VMEM((32, ROWS), BF16),
            pltpu.VMEM((HEADS * HEAD, 32), BF16),
            pltpu.VMEM((2, ROWS, HEAD), F32),
            pltpu.VMEM((2, ROWS, HEAD), F32),
            pltpu.VMEM((32, ROWS), BF16),
            pltpu.VMEM((4, 32, ROWS), BF16),
            pltpu.VMEM((2, 2, ROWS, HEAD), BF16),
            pltpu.VMEM((2, 2, ROWS, HEAD), BF16),
            pltpu.VMEM((8, 32, HEAD), BF16),
            pltpu.VMEM((8, 32, HEAD), BF16),
            pltpu.VMEM((8, 32, HEAD), BF16),
            pltpu.VMEM((8, 32, HEAD), BF16),
            pltpu.VMEM((8, 64, HEAD), BF16),
            pltpu.VMEM((8, 64, HEAD), BF16),
            pltpu.VMEM((4, 8, 32, HEAD), BF16),
            pltpu.SemaphoreType.DMA((8,)),
            pltpu.SemaphoreType.DMA((5,)),
            pltpu.SemaphoreType.DMA((COPIES,)),
            pltpu.SemaphoreType.DMA((COPIES,)),
        ],
        compiler_params=pltpu.CompilerParams(
            collective_id=0, has_side_effects=True, vmem_limit_bytes=56 * 1024 * 1024
        ),
    )(
        queries,
        keys,
        values,
        output_gradient,
        output_weight,
        adapter_down.T,
        adapter_up,
        jnp.broadcast_to(FREQUENCY[:, None], (64, HEAD)),
        positions[None, :],
        block_pair_mask,
    )
    dq, dk, dv, a, b = pl.pallas_call(
        write_kernel,
        out_shape=(
            out((ROWS, HEADS * HEAD), BF16),
            out((ROWS, 2 * HEAD), BF16),
            out((ROWS, 2 * HEAD), BF16),
            out((32, HEADS * HEAD), F32),
            out((32, WIDTH), F32),
        ),
        in_specs=[hbm] * 5,
        out_specs=(hbm,) * 5,
        scratch_shapes=[
            pltpu.VMEM((ROWS, HEADS * HEAD), BF16),
            pltpu.VMEM((ROWS, 2 * HEAD), BF16),
            pltpu.VMEM((ROWS, 2 * HEAD), BF16),
            pltpu.VMEM((32, HEADS * HEAD), F32),
            pltpu.VMEM((4, 8, 32, HEAD), BF16),
            pltpu.VMEM((32, WIDTH), F32),
            pltpu.SemaphoreType.DMA((8,)),
            pltpu.SemaphoreType.DMA((8,)),
        ],
    )(dq, dk, dv, a, b)
    return dq, dk, dv, a.T, b


def solution(mesh):
    placed = (
        P("seq", "rep"),
        P("seq", "rep"),
        P("seq", "rep"),
        P("seq", None),
        P("rep", None),
        P("rep", None),
        P(),
        P("seq"),
        P("seq", None, None, None),
    )
    return jax.shard_map(
        shards,
        mesh=mesh,
        in_specs=placed,
        out_specs=(P("seq", "rep"), P("seq", "rep"), P("seq", "rep"), P("rep", None), P()),
        check_vma=False,
    )
```

```python
import jax
import jax.numpy as jnp
import numpy as np
from jax import lax
from jax.experimental import pallas as pl
from jax.experimental.pallas import tpu as pltpu
from jax.sharding import PartitionSpec as P

HEAD = 128
ROWS = 512
HALF = 256
HEADS = 8
WIDTH = 4096
MESH = pl.DeviceIdType.MESH
F32 = jnp.float32
BF16 = jnp.bfloat16
SCALE = HEAD**-0.5
POWER = SCALE * 1.4426950408889634
HIDDEN = -1e30
AT_ONCE = 4
FREQUENCY = (1000000.0 ** (-np.arange(64) * 2.0 / 128)).astype(np.float32)

K_NEXT, V_NEXT, MID, RS1A, RS1B, ALLJ, AG2, BACK, AG3, COPIES = 0, 2, 4, 8, 16, 24, 32, 40, 42, 74


def dot(a, b):
    return jnp.dot(a, b, preferred_element_type=F32)


def dot_nt(a, b):
    return lax.dot_general(a, b, (((1,), (1,)), ((), ())), preferred_element_type=F32)


def seq_at(j, z):
    return (j // 4) * 32 + z * 4 + j % 4


def layer_kernel(
    q_hbm, k_hbm, v_hbm, og_hbm, w_hbm, down_hbm, up_hbm, freq, pos_row, codes,
    dq_hbm, dk_hbm, dv_hbm, a_hbm, b_out,
    k_nat, up, down_t, angle, dq_out, dk_out, dv_out, a_out,
    q_nat, og, w, k_all, v_all, k_t, v_t, q_t, diag, weights, stats, attn_own, attn_t, d_attn_t, back_t, down,
    dk_acc, dv_acc, mid_own, mid_all, back_send, back_recv,
    part_a, part_b, rs1a, rs1b, all_j, full, b_all,
    load_sem, store_sem, send_sem, recv_sem,
):
    s, r = lax.axis_index("seq"), lax.axis_index("rep")
    z, j = (s // 4) % 8, (s // 32) * 4 + s % 4
    along_z = [(seq_at(j, (z + o) % 8), r) for o in range(8)]
    along_j = [(seq_at((j + o) % 8, z), r) for o in range(8)]
    along_r = [(s, (r + o) % 4) for o in range(4)]
    after, before = ((s + 1) % 64, r), ((s + 63) % 64, r)
    peers = along_z[1:] + along_j[1:] + along_r[1:] + [after, before]

    def remote(at, src, dst, device):
        return pltpu.make_async_remote_copy(
            src_ref=src, dst_ref=dst, send_sem=send_sem.at[at], recv_sem=recv_sem.at[at],
            device_id=device, device_id_type=MESH,
        )

    def next_v(g):
        return remote(V_NEXT + g, v_all.at[g, 0:ROWS], v_all.at[g, ROWS : 2 * ROWS], after)

    def next_k(g):
        return remote(K_NEXT + g, k_all.at[g, 0:ROWS], k_all.at[g, ROWS : 2 * ROWS], after)

    def mids():
        return [remote(MID + o, mid_own, mid_all.at[o], along_r[o]) for o in range(1, 4)]

    def rs1_a():
        return [
            remote(RS1A + o, part_a.at[(z + o) % 8], rs1a.at[o], along_z[o]) for o in range(1, 8)
        ]

    def rs1_b():
        return [
            remote(RS1B + o, part_b.at[(z + o) % 8], rs1b.at[o], along_z[o]) for o in range(1, 8)
        ]

    def all_j_copies():
        return [remote(ALLJ + o, all_j.at[j], all_j.at[j], along_j[o]) for o in range(1, 8)]

    def ag2(o):
        return remote(AG2 + o, full.at[z], full.at[z], along_z[o])

    def ag3(k):
        block = full.at[(z + 8 - k) % 8, 32:64]
        land = b_all.at[r, (z + 8 - k) % 8]
        return [remote(AG3 + k * 4 + o, block, land, along_r[o]) for o in range(1, 4)]

    def back_copy(g):
        return remote(BACK + g, back_send.at[g], back_recv.at[g], before)

    def begin(copies):
        for copy in copies:
            copy.start()

    def finish(copies):
        for copy in copies:
            copy.wait()

    barrier = pltpu.get_barrier_semaphore()
    for p in peers:
        pl.semaphore_signal(barrier, inc=1, device_id=p, device_id_type=MESH)
    loads = []
    for at, (src, dst) in enumerate([
        (v_hbm.at[:, 0:HEAD], v_all.at[0, 0:ROWS]),
        (v_hbm.at[:, HEAD : 2 * HEAD], v_all.at[1, 0:ROWS]),
        (k_hbm, k_nat), (q_hbm, q_nat), (og_hbm, og), (up_hbm, up), (down_hbm, down_t), (w_hbm, w),
    ]):
        loads.append(pltpu.make_async_copy(src, dst, load_sem.at[at]))
        loads[at].start()
    load_v0, load_v1, load_k, load_q, load_og, load_up, load_down, load_w = loads

    load_v0.wait()
    pl.semaphore_wait(barrier, len(peers))
    next_v(0).start()
    q_pos = pos_row[...].astype(F32)
    phase = freq[:, 0:1] * q_pos
    angle[0] = jnp.cos(phase)
    angle[1] = jnp.sin(phase)
    cosine, sine = angle[0], angle[1]

    def turned(x):
        x1, x2 = x[:64], x[64:]
        return jnp.concatenate([x1 * cosine - x2 * sine, x2 * cosine + x1 * sine], 0)

    load_k.wait()
    for g in range(2):
        k_turned = turned(k_nat[:, g * HEAD : (g + 1) * HEAD].astype(F32).T)
        k_t[g, :, 0:ROWS] = k_turned.astype(BF16)
        k_all[g, 0:ROWS] = k_turned.T.astype(BF16)
        if g == 0:
            next_k(0).start()
    load_v1.wait()
    for g in range(2):
        v_t[g, :, 0:ROWS] = v_all[g, 0:ROWS].astype(F32).T.astype(BF16)

    k_pos = jnp.broadcast_to(q_pos, (8, ROWS)).T[:, 0:1]

    def hidden(step, a, b):
        return jnp.where(codes[0, step, a, b] == 1, 0.0, HIDDEN).astype(F32)

    for a in range(2):
        code = codes[0, 0, a, a]
        early = k_pos[a * HALF : (a + 1) * HALF] <= q_pos[:, a * HALF : (a + 1) * HALF]
        shown = jnp.where(early, jnp.where(code >= 1, 0.0, HIDDEN), jnp.where(code == 1, 0.0, HIDDEN))
        diag[a] = shown.astype(F32)

    load_q.wait()

    def turn_queries(h, carry):
        x = q_nat[:, pl.ds(pl.multiple_of(h * HEAD, HEAD), HEAD)].astype(F32).T
        q_t[h] = turned(x).astype(BF16)
        return carry

    lax.fori_loop(0, HEADS, turn_queries, 0)

    def forward_own(i, carry):
        heads = [i * AT_ONCE + u for u in range(AT_ONCE)]
        g = heads[0] // 4

        raws = [dot(k_all[g, 0:ROWS], q_t[h]) for h in heads]
        rounded = []
        for h, raw in zip(heads, raws):
            columns = []
            for a in range(2):
                cols = slice(a * HALF, (a + 1) * HALF)
                same = raw[cols, cols] + diag[a]
                other = raw[(1 - a) * HALF : (2 - a) * HALF, cols]
                off = hidden(0, a, 1 - a)
                top = jnp.maximum(
                    jnp.max(same, 0, keepdims=True), jnp.max(other, 0, keepdims=True) + off
                )
                shift = top * -POWER
                same = jnp.exp2(same * POWER + shift)
                other = jnp.exp2(other * POWER + (shift + off))
                total = jnp.sum(same, 0, keepdims=True) + jnp.sum(other, 0, keepdims=True)
                stats[h, 0:1, cols] = top
                stats[h, 1:2, cols] = total
                pair = [same, other] if a == 0 else [other, same]
                columns.append(jnp.concatenate(pair, 0).astype(BF16))
            rounded.append(jnp.concatenate(columns, 1))
        for h, e in zip(heads, rounded):
            weights[h, 0:ROWS] = e
            attn_own[h] = dot(v_t[g, :, 0:ROWS], e)
        return carry

    lax.fori_loop(0, HEADS // AT_ONCE, forward_own, 0)

    next_v(0).wait_send()
    next_k(0).wait_send()
    next_k(1).start()
    load_og.wait()
    load_up.wait()
    load_down.wait()
    back_t[...] = dot_nt(up[...], og[...]).astype(BF16)
    down[...] = down_t[...].astype(F32).T.astype(BF16)
    load_w.wait()

    def project(i, carry):
        at = pl.multiple_of(i * 512, 512)
        x = dot_nt(w[pl.ds(at, 512)], og[...]) + 2.0 * dot(down[pl.ds(at, 512)], back_t[...])
        d_attn_t[pl.ds(i * 4, 4)] = x.astype(BF16).reshape(4, HEAD, ROWS)
        return carry

    project(0, 0)
    next_k(1).wait_send()
    next_v(1).start()

    def previous_scores(g):
        heads = range(g * 4, g * 4 + 4)
        raws = [dot(k_all[g, ROWS : 2 * ROWS], q_t[h]) for h in heads]
        for h, raw in zip(heads, raws):
            columns = []
            for a in range(2):
                cols = slice(a * HALF, (a + 1) * HALF)
                first, second = raw[0:HALF, cols], raw[HALF:ROWS, cols]
                off1, off2 = hidden(1, a, 0), hidden(1, a, 1)
                top = jnp.maximum(
                    jnp.max(first, 0, keepdims=True) + off1, jnp.max(second, 0, keepdims=True) + off2
                )
                shift = jnp.minimum(top * -POWER, 1e28)
                first = jnp.exp2(first * POWER + (shift + off1))
                second = jnp.exp2(second * POWER + (shift + off2))
                total = jnp.sum(first, 0, keepdims=True) + jnp.sum(second, 0, keepdims=True)
                top_own = stats[h, 0:1, cols]
                top_all = jnp.maximum(top, top_own)
                own = jnp.exp2((top_own - top_all) * POWER)
                previous = jnp.exp2((top - top_all) * POWER)
                share = 1.0 / (stats[h, 1:2, cols] * own + total * previous)
                own, previous = own * share, previous * share
                stats[h, 2:3, cols] = own
                stats[h, 3:4, cols] = previous
                columns.append(jnp.concatenate([first, second], 0).astype(BF16))
            weights[h, ROWS : 2 * ROWS] = jnp.concatenate(columns, 1)

    def previous_values(g):
        v_t[g, :, ROWS : 2 * ROWS] = v_all[g, ROWS : 2 * ROWS].astype(F32).T.astype(BF16)
        for h in range(g * 4, g * 4 + 4):
            part = dot(v_t[g, :, ROWS : 2 * ROWS], weights[h, ROWS : 2 * ROWS])
            attn_t[h] = (attn_own[h] * stats[h, 2:3] + part * stats[h, 3:4]).astype(BF16)

    next_k(0).wait_recv()
    next_v(0).wait_recv()
    previous_scores(0)
    previous_values(0)
    next_k(1).wait_recv()
    previous_scores(1)
    next_v(1).wait()
    previous_values(1)

    mid_part = dot(down_t[...], attn_t[...].reshape(HEADS * HEAD, ROWS))
    mid_own[...] = mid_part.astype(BF16)
    begin(mids())
    for h in range(HEADS):
        part_a[h] = dot_nt(back_t[...], attn_t[h]).astype(BF16)
    begin(rs1_a())

    def backward(t, g):
        rows = slice(t * ROWS, (t + 1) * ROWS)
        heads = range(g * 4, g * 4 + 4)
        d_weights = [dot(v_all[g, rows], d_attn_t[h]) for h in heads]
        d_scores, scaled = [], []
        for h, d_weight in zip(heads, d_weights):
            grad = d_attn_t[h].astype(F32)
            factor = stats[h, 2 + t : 3 + t]
            if t == 1:
                stats[h, 4:5] = jnp.sum(grad * attn_t[h].astype(F32), 0, keepdims=True)
            delta = stats[h, 4:5]
            p = weights[h, rows].astype(F32)
            d_scores.append((p * (d_weight * factor - delta * factor)).astype(BF16))
            scaled.append((grad * factor).astype(BF16))
        dk = [dot_nt(x, q_t[h]) for h, x in zip(heads, d_scores)]
        dv = [dot_nt(weights[h, rows], x) for h, x in zip(heads, scaled)]
        dk, dv = sum(dk[1:], dk[0]) * SCALE, sum(dv[1:], dv[0])
        if t == 1:
            back_send[g, 0] = dk.astype(BF16)
            back_send[g, 1] = dv.astype(BF16)
        else:
            dk_acc[g] = dk
            dv_acc[g] = dv
        for h, x in zip(heads, d_scores):
            dq = dot(k_t[g, :, rows], x)
            if t == 1:
                attn_own[h] = dq
            else:
                dq = (dq + attn_own[h]) * SCALE
                x1, x2 = dq[:64], dq[64:]
                dq = jnp.concatenate([x1 * cosine + x2 * sine, x2 * cosine - x1 * sine], 0)
                dq_out[:, h * HEAD : (h + 1) * HEAD] = dq.T.astype(BF16)

    def finish_keys(g):
        back_copy(g).wait()
        x = (dk_acc[g] + back_recv[g, 0].astype(F32)).T
        x1, x2 = x[:64], x[64:]
        x = jnp.concatenate([x1 * cosine + x2 * sine, x2 * cosine - x1 * sine], 0)
        dk_out[:, g * HEAD : (g + 1) * HEAD] = x.T.astype(BF16)
        dv = dv_acc[g] + back_recv[g, 1].astype(F32)
        dv_out[:, g * HEAD : (g + 1) * HEAD] = dv.astype(BF16)

    stores = [
        pltpu.make_async_copy(src, dst, store_sem.at[i])
        for i, (src, dst) in enumerate([
            (dq_out.at[:, 0:512], dq_hbm.at[:, 0:512]),
            (dq_out.at[:, 512:1024], dq_hbm.at[:, 512:1024]),
            (dk_out, dk_hbm), (dv_out, dv_hbm), (a_out, a_hbm),
        ])
    ]

    for g in range(2):
        k_t[g, :, ROWS : 2 * ROWS] = k_all[g, ROWS : 2 * ROWS].astype(F32).T.astype(BF16)
    backward(1, 0)
    back_copy(0).start()
    finish(mids())
    mid = mid_part
    for o in range(1, 4):
        mid = mid + mid_all[o].astype(F32)
    b_part = dot(mid.astype(BF16), og[:, pl.ds(pl.multiple_of(r * 1024, 1024), 1024)])
    for c in range(8):
        part_b[c] = b_part[:, c * HEAD : (c + 1) * HEAD].astype(BF16)
    begin(rs1_b())

    project(1, 0)
    finish(rs1_a())
    finish(rs1_b())
    total_a, total_b = part_a[z].astype(F32), part_b[z].astype(F32)
    for o in range(1, 8):
        total_a = total_a + rs1a[o].astype(F32)
        total_b = total_b + rs1b[o].astype(F32)
    all_j[j, 0:32] = total_a.astype(BF16)
    all_j[j, 32:64] = total_b.astype(BF16)
    begin(all_j_copies())

    backward(1, 1)
    finish(all_j_copies())
    total = all_j[0].astype(F32)
    for o in range(1, 8):
        total = total + all_j[o].astype(F32)
    full[z] = (2.0 * total).astype(BF16)
    begin([ag2(o) for o in range(1, 8)])
    begin(ag3(0))
    back_copy(1).start()

    backward(0, 0)
    stores[0].start()
    for o in range(1, 8):
        ag2(o).wait()
        begin(ag3(o))
    b_all[r] = full[:, 32:64, :]
    for c in range(8):
        a_out[:, c * HEAD : (c + 1) * HEAD] = full[c, 0:32].astype(F32)
    stores[4].start()
    backward(0, 1)
    stores[1].start()
    finish_keys(0)
    finish_keys(1)
    stores[2].start()
    stores[3].start()
    for k in range(8):
        finish(ag3(k))
    b_out[...] = b_all[...]
    finish(stores)


def write_kernel(
    dq, dk, dv, a, b, dq_out, dk_out, dv_out, a_out, b_out,
    dq_in, dk_in, dv_in, a_in, b_in, b_wide, in_sem, out_sem,
):
    quarter = ROWS // 4
    steps = [(dk, dk_in, dk_out), (dv, dv_in, dv_out), (a, a_in, a_out)]
    for i in range(4):
        rows = slice(i * quarter, (i + 1) * quarter)
        steps.append((dq.at[rows], dq_in.at[rows], dq_out.at[rows]))
    loads = [pltpu.make_async_copy(x, y, in_sem.at[i]) for i, (x, y, _) in enumerate(steps)]
    stores = [pltpu.make_async_copy(y, o, out_sem.at[i]) for i, (_, y, o) in enumerate(steps)]
    load_b = pltpu.make_async_copy(b, b_in, in_sem.at[7])
    store_b = pltpu.make_async_copy(b_wide, b_out, out_sem.at[7])
    load_b.start()
    for copy in loads:
        copy.start()
    load_b.wait()
    for p in range(4):
        for c in range(8):
            at = p * 1024 + c * HEAD
            b_wide[:, at : at + HEAD] = b_in[p, c].astype(F32)
    store_b.start()
    for load, store in zip(loads, stores):
        load.wait()
        store.start()
    for copy in stores:
        copy.wait()
    store_b.wait()


def shards(
    queries,
    keys,
    values,
    output_gradient,
    output_weight,
    adapter_down,
    adapter_up,
    positions,
    block_pair_mask,
):
    vmem = pl.BlockSpec(memory_space=pltpu.VMEM)
    smem = pl.BlockSpec(memory_space=pltpu.SMEM)
    hbm = pl.BlockSpec(memory_space=pl.ANY)
    out = jax.ShapeDtypeStruct
    dq, dk, dv, a, b = pl.pallas_call(
        layer_kernel,
        out_shape=(
            out((ROWS, HEADS * HEAD), BF16),
            out((ROWS, 2 * HEAD), BF16),
            out((ROWS, 2 * HEAD), BF16),
            out((32, HEADS * HEAD), F32),
            out((4, 8, 32, HEAD), BF16),
        ),
        in_specs=[hbm] * 7 + [vmem, vmem, smem],
        out_specs=(hbm,) * 4 + (vmem,),
        scratch_shapes=[
            pltpu.VMEM((ROWS, 2 * HEAD), BF16),
            pltpu.VMEM((32, WIDTH), BF16),
            pltpu.VMEM((32, HEADS * HEAD), BF16),
            pltpu.VMEM((2, 64, ROWS), F32),
            pltpu.VMEM((ROWS, HEADS * HEAD), BF16),
            pltpu.VMEM((ROWS, 2 * HEAD), BF16),
            pltpu.VMEM((ROWS, 2 * HEAD), BF16),
            pltpu.VMEM((32, HEADS * HEAD), F32),
            pltpu.VMEM((ROWS, HEADS * HEAD), BF16),
            pltpu.VMEM((ROWS, WIDTH), BF16),
            pltpu.VMEM((HEADS * HEAD, WIDTH), BF16),
            pltpu.VMEM((2, 2 * ROWS, HEAD), BF16),
            pltpu.VMEM((2, 2 * ROWS, HEAD), BF16),
            pltpu.VMEM((2, HEAD, 2 * ROWS), BF16),
            pltpu.VMEM((2, HEAD, 2 * ROWS), BF16),
            pltpu.VMEM((HEADS, HEAD, ROWS), BF16),
            pltpu.VMEM((2, HALF, HALF), F32),
            pltpu.VMEM((HEADS, 2 * ROWS, ROWS), BF16),
            pltpu.VMEM((HEADS, 8, ROWS), F32),
            pltpu.VMEM((HEADS, HEAD, ROWS), F32),
            pltpu.VMEM((HEADS, HEAD, ROWS), BF16),
            pltpu.VMEM((HEADS, HEAD, ROWS), BF16),
            pltpu.VMEM((32, ROWS), BF16),
            pltpu.VMEM((HEADS * HEAD, 32), BF16),
            pltpu.VMEM((2, ROWS, HEAD), F32),
            pltpu.VMEM((2, ROWS, HEAD), F32),
            pltpu.VMEM((32, ROWS), BF16),
            pltpu.VMEM((4, 32, ROWS), BF16),
            pltpu.VMEM((2, 2, ROWS, HEAD), BF16),
            pltpu.VMEM((2, 2, ROWS, HEAD), BF16),
            pltpu.VMEM((8, 32, HEAD), BF16),
            pltpu.VMEM((8, 32, HEAD), BF16),
            pltpu.VMEM((8, 32, HEAD), BF16),
            pltpu.VMEM((8, 32, HEAD), BF16),
            pltpu.VMEM((8, 64, HEAD), BF16),
            pltpu.VMEM((8, 64, HEAD), BF16),
            pltpu.VMEM((4, 8, 32, HEAD), BF16),
            pltpu.SemaphoreType.DMA((8,)),
            pltpu.SemaphoreType.DMA((5,)),
            pltpu.SemaphoreType.DMA((COPIES,)),
            pltpu.SemaphoreType.DMA((COPIES,)),
        ],
        compiler_params=pltpu.CompilerParams(
            collective_id=0, has_side_effects=True, vmem_limit_bytes=56 * 1024 * 1024
        ),
    )(
        queries,
        keys,
        values,
        output_gradient,
        output_weight,
        adapter_down.T,
        adapter_up,
        jnp.broadcast_to(FREQUENCY[:, None], (64, HEAD)),
        positions[None, :],
        block_pair_mask,
    )
    dq, dk, dv, a, b = pl.pallas_call(
        write_kernel,
        out_shape=(
            out((ROWS, HEADS * HEAD), BF16),
            out((ROWS, 2 * HEAD), BF16),
            out((ROWS, 2 * HEAD), BF16),
            out((32, HEADS * HEAD), F32),
            out((32, WIDTH), F32),
        ),
        in_specs=[hbm] * 5,
        out_specs=(hbm,) * 5,
        scratch_shapes=[
            pltpu.VMEM((ROWS, HEADS * HEAD), BF16),
            pltpu.VMEM((ROWS, 2 * HEAD), BF16),
            pltpu.VMEM((ROWS, 2 * HEAD), BF16),
            pltpu.VMEM((32, HEADS * HEAD), F32),
            pltpu.VMEM((4, 8, 32, HEAD), BF16),
            pltpu.VMEM((32, WIDTH), F32),
            pltpu.SemaphoreType.DMA((8,)),
            pltpu.SemaphoreType.DMA((8,)),
        ],
    )(dq, dk, dv, a, b)
    return dq, dk, dv, a.T, b


def solution(mesh):
    placed = (
        P("seq", "rep"),
        P("seq", "rep"),
        P("seq", "rep"),
        P("seq", None),
        P("rep", None),
        P("rep", None),
        P(),
        P("seq"),
        P("seq", None, None, None),
    )
    return jax.shard_map(
        shards,
        mesh=mesh,
        in_specs=placed,
        out_specs=(P("seq", "rep"), P("seq", "rep"), P("seq", "rep"), P("rep", None), P()),
        check_vma=False,
    )
```

```python
import jax
import jax.numpy as jnp
import numpy as np
from jax import lax
from jax.experimental import pallas as pl
from jax.experimental.pallas import tpu as pltpu
from jax.sharding import PartitionSpec as P

HEAD = 128
ROWS = 512
HALF = 256
HEADS = 8
WIDTH = 4096
MESH = pl.DeviceIdType.MESH
F32 = jnp.float32
BF16 = jnp.bfloat16
SCALE = HEAD**-0.5
POWER = SCALE * 1.4426950408889634
HIDDEN = -1e30
AT_ONCE = 4
FREQUENCY = [float(np.float32(1000000.0 ** (-i * 2.0 / 128))) for i in range(64)]

K_NEXT, V_NEXT, MID, RS1A, RS1B, ALLJ, AG2, BACK, AG3, COPIES = 0, 2, 4, 8, 16, 24, 32, 40, 42, 74


def dot(a, b):
    return jnp.dot(a, b, preferred_element_type=F32)


def dot_nt(a, b):
    return lax.dot_general(a, b, (((1,), (1,)), ((), ())), preferred_element_type=F32)


def seq_at(j, z):
    return (j // 4) * 32 + z * 4 + j % 4


def layer_kernel(
    q_hbm, k_hbm, v_hbm, og_hbm, w_hbm, down_hbm, up_hbm, pos_hbm, codes_hbm,
    dq_hbm, dk_hbm, dv_hbm, a_hbm, b_hbm,
    pos_row, codes, k_nat, up, down_t, angle, dq_out, dk_out, dv_out, a_out,
    q_nat, og, w, k_all, v_all, k_t, v_t, q_t, diag, weights, stats, attn_own, attn_t, d_attn_t, back_t, down,
    dk_acc, dv_acc, mid_own, mid_all, back_send, back_recv,
    part_a, part_b, rs1a, rs1b, all_j, full, b_all,
    load_sem, store_sem, send_sem, recv_sem,
):
    s, r = lax.axis_index("seq"), lax.axis_index("rep")
    z, j = (s // 4) % 8, (s // 32) * 4 + s % 4
    along_z = [(seq_at(j, (z + o) % 8), r) for o in range(8)]
    along_j = [(seq_at((j + o) % 8, z), r) for o in range(8)]
    along_r = [(s, (r + o) % 4) for o in range(4)]
    after, before = ((s + 1) % 64, r), ((s + 63) % 64, r)
    peers = along_z[1:] + along_j[1:] + along_r[1:] + [after, before]

    def remote(at, src, dst, device):
        return pltpu.make_async_remote_copy(
            src_ref=src, dst_ref=dst, send_sem=send_sem.at[at], recv_sem=recv_sem.at[at],
            device_id=device, device_id_type=MESH,
        )

    def next_v(g):
        return remote(V_NEXT + g, v_all.at[g, 0:ROWS], v_all.at[g, ROWS : 2 * ROWS], after)

    def next_k(g):
        return remote(K_NEXT + g, k_all.at[g, 0:ROWS], k_all.at[g, ROWS : 2 * ROWS], after)

    def mids():
        return [remote(MID + o, mid_own, mid_all.at[o], along_r[o]) for o in range(1, 4)]

    def rs1_a():
        return [
            remote(RS1A + o, part_a.at[(z + o) % 8], rs1a.at[o], along_z[o]) for o in range(1, 8)
        ]

    def rs1_b():
        return [
            remote(RS1B + o, part_b.at[(z + o) % 8], rs1b.at[o], along_z[o]) for o in range(1, 8)
        ]

    def all_j_copies():
        return [remote(ALLJ + o, all_j.at[j], all_j.at[j], along_j[o]) for o in range(1, 8)]

    def ag2(o):
        return remote(AG2 + o, full.at[z], full.at[z], along_z[o])

    def ag3(k):
        block = full.at[(z + 8 - k) % 8, 32:64]
        land = b_all.at[r, (z + 8 - k) % 8]
        return [remote(AG3 + k * 4 + o, block, land, along_r[o]) for o in range(1, 4)]

    def back_copy(g):
        return remote(BACK + g, back_send.at[g], back_recv.at[g], before)

    def begin(copies):
        for copy in copies:
            copy.start()

    def finish(copies):
        for copy in copies:
            copy.wait()

    barrier = pltpu.get_barrier_semaphore()
    for p in peers:
        pl.semaphore_signal(barrier, inc=1, device_id=p, device_id_type=MESH)
    loads = []
    for at, (src, dst) in enumerate([
        (v_hbm.at[:, 0:HEAD], v_all.at[0, 0:ROWS]),
        (v_hbm.at[:, HEAD : 2 * HEAD], v_all.at[1, 0:ROWS]),
        (pos_hbm, pos_row), (codes_hbm, codes), (k_hbm, k_nat), (q_hbm, q_nat), (og_hbm, og), (up_hbm, up), (down_hbm, down_t), (w_hbm, w),
    ]):
        loads.append(pltpu.make_async_copy(src, dst, load_sem.at[at]))
        loads[at].start()
    load_v0, load_v1, load_pos, load_codes, load_k, load_q, load_og, load_up, load_down, load_w = loads

    row = lax.broadcasted_iota(jnp.int32, (64, HEAD), 0)
    freq = jnp.zeros((64, HEAD), F32)
    for i in range(64):
        freq = jnp.where(row == i, FREQUENCY[i], freq)
    load_v0.wait()
    pl.semaphore_wait(barrier, len(peers))
    next_v(0).start()
    load_pos.wait()
    q_pos = pos_row[...].astype(F32)
    phase = freq[:, 0:1] * q_pos
    angle[0] = jnp.cos(phase)
    angle[1] = jnp.sin(phase)
    cosine, sine = angle[0], angle[1]

    def turned(x):
        x1, x2 = x[:64], x[64:]
        return jnp.concatenate([x1 * cosine - x2 * sine, x2 * cosine + x1 * sine], 0)

    load_k.wait()
    for g in range(2):
        k_turned = turned(k_nat[:, g * HEAD : (g + 1) * HEAD].astype(F32).T)
        k_t[g, :, 0:ROWS] = k_turned.astype(BF16)
        k_all[g, 0:ROWS] = k_turned.T.astype(BF16)
        next_k(g).start()
    load_v1.wait()
    for g in range(2):
        v_t[g, :, 0:ROWS] = v_all[g, 0:ROWS].astype(F32).T.astype(BF16)

    load_codes.wait()
    k_pos = jnp.broadcast_to(q_pos, (8, ROWS)).T[:, 0:1]

    def hidden(step, a, b):
        return jnp.where(codes[0, step, a, b] == 1, 0.0, HIDDEN).astype(F32)

    for a in range(2):
        code = codes[0, 0, a, a]
        early = k_pos[a * HALF : (a + 1) * HALF] <= q_pos[:, a * HALF : (a + 1) * HALF]
        shown = jnp.where(early, jnp.where(code >= 1, 0.0, HIDDEN), jnp.where(code == 1, 0.0, HIDDEN))
        diag[a] = shown.astype(F32)

    load_q.wait()

    def turn_queries(h, carry):
        x = q_nat[:, pl.ds(pl.multiple_of(h * HEAD, HEAD), HEAD)].astype(F32).T
        q_t[h] = turned(x).astype(BF16)
        return carry

    lax.fori_loop(0, HEADS, turn_queries, 0)

    def forward_own(i, carry):
        heads = [i * AT_ONCE + u for u in range(AT_ONCE)]
        g = heads[0] // 4

        raws = [dot(k_all[g, 0:ROWS], q_t[h]) for h in heads]
        rounded = []
        for h, raw in zip(heads, raws):
            columns = []
            for a in range(2):
                cols = slice(a * HALF, (a + 1) * HALF)
                same = raw[cols, cols] + diag[a]
                other = raw[(1 - a) * HALF : (2 - a) * HALF, cols]
                off = hidden(0, a, 1 - a)
                top = jnp.maximum(
                    jnp.max(same, 0, keepdims=True), jnp.max(other, 0, keepdims=True) + off
                )
                shift = top * -POWER
                same = jnp.exp2(same * POWER + shift)
                other = jnp.exp2(other * POWER + (shift + off))
                total = jnp.sum(same, 0, keepdims=True) + jnp.sum(other, 0, keepdims=True)
                stats[h, 0:1, cols] = top
                stats[h, 1:2, cols] = total
                pair = [same, other] if a == 0 else [other, same]
                columns.append(jnp.concatenate(pair, 0).astype(BF16))
            rounded.append(jnp.concatenate(columns, 1))
        for h, e in zip(heads, rounded):
            weights[h, 0:ROWS] = e
            attn_own[h] = dot(v_t[g, :, 0:ROWS], e)
        return carry

    lax.fori_loop(0, HEADS // AT_ONCE, forward_own, 0)

    next_v(1).start()
    load_og.wait()
    load_up.wait()
    load_down.wait()
    back_t[...] = dot_nt(up[...], og[...]).astype(BF16)
    down[...] = down_t[...].astype(F32).T.astype(BF16)
    load_w.wait()

    def project(i, carry):
        at = pl.multiple_of(i * 512, 512)
        x = dot_nt(w[pl.ds(at, 512)], og[...]) + 2.0 * dot(down[pl.ds(at, 512)], back_t[...])
        d_attn_t[pl.ds(i * 4, 4)] = x.astype(BF16).reshape(4, HEAD, ROWS)
        return carry

    project(0, 0)

    def previous_scores(g):
        heads = range(g * 4, g * 4 + 4)
        raws = [dot(k_all[g, ROWS : 2 * ROWS], q_t[h]) for h in heads]
        for h, raw in zip(heads, raws):
            columns = []
            for a in range(2):
                cols = slice(a * HALF, (a + 1) * HALF)
                first, second = raw[0:HALF, cols], raw[HALF:ROWS, cols]
                off1, off2 = hidden(1, a, 0), hidden(1, a, 1)
                top = jnp.maximum(
                    jnp.max(first, 0, keepdims=True) + off1, jnp.max(second, 0, keepdims=True) + off2
                )
                shift = jnp.minimum(top * -POWER, 1e28)
                first = jnp.exp2(first * POWER + (shift + off1))
                second = jnp.exp2(second * POWER + (shift + off2))
                total = jnp.sum(first, 0, keepdims=True) + jnp.sum(second, 0, keepdims=True)
                top_own = stats[h, 0:1, cols]
                top_all = jnp.maximum(top, top_own)
                own = jnp.exp2((top_own - top_all) * POWER)
                previous = jnp.exp2((top - top_all) * POWER)
                share = 1.0 / (stats[h, 1:2, cols] * own + total * previous)
                own, previous = own * share, previous * share
                stats[h, 2:3, cols] = own
                stats[h, 3:4, cols] = previous
                columns.append(jnp.concatenate([first, second], 0).astype(BF16))
            weights[h, ROWS : 2 * ROWS] = jnp.concatenate(columns, 1)

    def previous_values(g):
        v_t[g, :, ROWS : 2 * ROWS] = v_all[g, ROWS : 2 * ROWS].astype(F32).T.astype(BF16)
        for h in range(g * 4, g * 4 + 4):
            part = dot(v_t[g, :, ROWS : 2 * ROWS], weights[h, ROWS : 2 * ROWS])
            attn_t[h] = (attn_own[h] * stats[h, 2:3] + part * stats[h, 3:4]).astype(BF16)

    next_k(0).wait()
    next_v(0).wait()
    previous_scores(0)
    previous_values(0)
    next_k(1).wait()
    previous_scores(1)
    next_v(1).wait()
    previous_values(1)

    mid_part = dot(down_t[...], attn_t[...].reshape(HEADS * HEAD, ROWS))
    mid_own[...] = mid_part.astype(BF16)
    begin(mids())
    for h in range(HEADS):
        part_a[h] = dot_nt(back_t[...], attn_t[h]).astype(BF16)
    begin(rs1_a())

    def backward(t, g):
        rows = slice(t * ROWS, (t + 1) * ROWS)
        heads = range(g * 4, g * 4 + 4)
        d_weights = [dot(v_all[g, rows], d_attn_t[h]) for h in heads]
        d_scores, scaled = [], []
        for h, d_weight in zip(heads, d_weights):
            grad = d_attn_t[h].astype(F32)
            factor = stats[h, 2 + t : 3 + t]
            if t == 1:
                stats[h, 4:5] = jnp.sum(grad * attn_t[h].astype(F32), 0, keepdims=True)
            delta = stats[h, 4:5]
            p = weights[h, rows].astype(F32)
            d_scores.append((p * (d_weight * factor - delta * factor)).astype(BF16))
            scaled.append((grad * factor).astype(BF16))
        dk = [dot_nt(x, q_t[h]) for h, x in zip(heads, d_scores)]
        dv = [dot_nt(weights[h, rows], x) for h, x in zip(heads, scaled)]
        dk, dv = sum(dk[1:], dk[0]) * SCALE, sum(dv[1:], dv[0])
        if t == 1:
            back_send[g, 0] = dk.astype(BF16)
            back_send[g, 1] = dv.astype(BF16)
        else:
            dk_acc[g] = dk
            dv_acc[g] = dv
        for h, x in zip(heads, d_scores):
            dq = dot(k_t[g, :, rows], x)
            if t == 1:
                attn_own[h] = dq
            else:
                dq = (dq + attn_own[h]) * SCALE
                x1, x2 = dq[:64], dq[64:]
                dq = jnp.concatenate([x1 * cosine + x2 * sine, x2 * cosine - x1 * sine], 0)
                dq_out[:, h * HEAD : (h + 1) * HEAD] = dq.T.astype(BF16)

    def finish_keys(g):
        back_copy(g).wait()
        x = (dk_acc[g] + back_recv[g, 0].astype(F32)).T
        x1, x2 = x[:64], x[64:]
        x = jnp.concatenate([x1 * cosine + x2 * sine, x2 * cosine - x1 * sine], 0)
        dk_out[:, g * HEAD : (g + 1) * HEAD] = x.T.astype(BF16)
        dv = dv_acc[g] + back_recv[g, 1].astype(F32)
        dv_out[:, g * HEAD : (g + 1) * HEAD] = dv.astype(BF16)

    stores = [
        pltpu.make_async_copy(src, dst, store_sem.at[i])
        for i, (src, dst) in enumerate([
            (dq_out.at[:, 0:512], dq_hbm.at[:, 0:512]),
            (dq_out.at[:, 512:1024], dq_hbm.at[:, 512:1024]),
            (dk_out, dk_hbm), (dv_out, dv_hbm), (a_out, a_hbm),
        ])
    ]

    for g in range(2):
        k_t[g, :, ROWS : 2 * ROWS] = k_all[g, ROWS : 2 * ROWS].astype(F32).T.astype(BF16)
    backward(1, 0)
    back_copy(0).start()
    finish(mids())
    mid = mid_part
    for o in range(1, 4):
        mid = mid + mid_all[o].astype(F32)
    b_part = dot(mid.astype(BF16), og[:, pl.ds(pl.multiple_of(r * 1024, 1024), 1024)])
    for c in range(8):
        part_b[c] = b_part[:, c * HEAD : (c + 1) * HEAD].astype(BF16)
    begin(rs1_b())

    project(1, 0)
    finish(rs1_a())
    finish(rs1_b())
    total_a, total_b = part_a[z].astype(F32), part_b[z].astype(F32)
    for o in range(1, 8):
        total_a = total_a + rs1a[o].astype(F32)
        total_b = total_b + rs1b[o].astype(F32)
    all_j[j, 0:32] = total_a.astype(BF16)
    all_j[j, 32:64] = total_b.astype(BF16)
    begin(all_j_copies())

    backward(1, 1)
    finish(all_j_copies())
    total = all_j[0].astype(F32)
    for o in range(1, 8):
        total = total + all_j[o].astype(F32)
    full[z] = (2.0 * total).astype(BF16)
    begin([ag2(o) for o in range(1, 8)])
    begin(ag3(0))
    back_copy(1).start()

    backward(0, 0)
    stores[0].start()
    for o in range(1, 8):
        ag2(o).wait()
        begin(ag3(o))
    b_all[r] = full[:, 32:64, :]
    for c in range(8):
        a_out[:, c * HEAD : (c + 1) * HEAD] = full[c, 0:32].astype(F32)
    stores[4].start()
    backward(0, 1)
    stores[1].start()
    finish_keys(0)
    finish_keys(1)
    stores[2].start()
    stores[3].start()
    for k in range(8):
        finish(ag3(k))
    store_b = pltpu.make_async_copy(b_all, b_hbm, store_sem.at[5])
    store_b.start()
    finish(stores)
    store_b.wait()


def write_kernel(
    dq, dk, dv, a, b, dq_out, dk_out, dv_out, a_out, b_out,
    dq_in, dk_in, dv_in, a_in, b_in, b_wide, in_sem, out_sem,
):
    quarter = ROWS // 4
    steps = [(dk, dk_in, dk_out), (dv, dv_in, dv_out), (a, a_in, a_out)]
    for i in range(4):
        rows = slice(i * quarter, (i + 1) * quarter)
        steps.append((dq.at[rows], dq_in.at[rows], dq_out.at[rows]))
    loads = [pltpu.make_async_copy(x, y, in_sem.at[i]) for i, (x, y, _) in enumerate(steps)]
    stores = [pltpu.make_async_copy(y, o, out_sem.at[i]) for i, (_, y, o) in enumerate(steps)]
    load_b = pltpu.make_async_copy(b, b_in, in_sem.at[7])
    store_b = pltpu.make_async_copy(b_wide, b_out, out_sem.at[7])
    load_b.start()
    for copy in loads:
        copy.start()
    load_b.wait()
    for p in range(4):
        for c in range(8):
            at = p * 1024 + c * HEAD
            b_wide[:, at : at + HEAD] = b_in[p, c].astype(F32)
    store_b.start()
    for load, store in zip(loads, stores):
        load.wait()
        store.start()
    for copy in stores:
        copy.wait()
    store_b.wait()


def shards(
    queries,
    keys,
    values,
    output_gradient,
    output_weight,
    adapter_down,
    adapter_up,
    positions,
    block_pair_mask,
):
    anywhere = pl.BlockSpec(memory_space=pl.ANY)
    hbm = pl.BlockSpec(memory_space=pl.ANY)
    out = jax.ShapeDtypeStruct
    dq, dk, dv, a, b = pl.pallas_call(
        layer_kernel,
        out_shape=(
            out((ROWS, HEADS * HEAD), BF16),
            out((ROWS, 2 * HEAD), BF16),
            out((ROWS, 2 * HEAD), BF16),
            out((32, HEADS * HEAD), F32),
            out((4, 8, 32, HEAD), BF16),
        ),
        in_specs=[hbm] * 9,
        out_specs=(anywhere,) * 5,
        scratch_shapes=[
            pltpu.VMEM((1, ROWS), jnp.int32),
            pltpu.SMEM((1, 2, 2, 2), jnp.int32),
            pltpu.VMEM((ROWS, 2 * HEAD), BF16),
            pltpu.VMEM((32, WIDTH), BF16),
            pltpu.VMEM((32, HEADS * HEAD), BF16),
            pltpu.VMEM((2, 64, ROWS), F32),
            pltpu.VMEM((ROWS, HEADS * HEAD), BF16),
            pltpu.VMEM((ROWS, 2 * HEAD), BF16),
            pltpu.VMEM((ROWS, 2 * HEAD), BF16),
            pltpu.VMEM((32, HEADS * HEAD), F32),
            pltpu.VMEM((ROWS, HEADS * HEAD), BF16),
            pltpu.VMEM((ROWS, WIDTH), BF16),
            pltpu.VMEM((HEADS * HEAD, WIDTH), BF16),
            pltpu.VMEM((2, 2 * ROWS, HEAD), BF16),
            pltpu.VMEM((2, 2 * ROWS, HEAD), BF16),
            pltpu.VMEM((2, HEAD, 2 * ROWS), BF16),
            pltpu.VMEM((2, HEAD, 2 * ROWS), BF16),
            pltpu.VMEM((HEADS, HEAD, ROWS), BF16),
            pltpu.VMEM((2, HALF, HALF), F32),
            pltpu.VMEM((HEADS, 2 * ROWS, ROWS), BF16),
            pltpu.VMEM((HEADS, 8, ROWS), F32),
            pltpu.VMEM((HEADS, HEAD, ROWS), F32),
            pltpu.VMEM((HEADS, HEAD, ROWS), BF16),
            pltpu.VMEM((HEADS, HEAD, ROWS), BF16),
            pltpu.VMEM((32, ROWS), BF16),
            pltpu.VMEM((HEADS * HEAD, 32), BF16),
            pltpu.VMEM((2, ROWS, HEAD), F32),
            pltpu.VMEM((2, ROWS, HEAD), F32),
            pltpu.VMEM((32, ROWS), BF16),
            pltpu.VMEM((4, 32, ROWS), BF16),
            pltpu.VMEM((2, 2, ROWS, HEAD), BF16),
            pltpu.VMEM((2, 2, ROWS, HEAD), BF16),
            pltpu.VMEM((8, 32, HEAD), BF16),
            pltpu.VMEM((8, 32, HEAD), BF16),
            pltpu.VMEM((8, 32, HEAD), BF16),
            pltpu.VMEM((8, 32, HEAD), BF16),
            pltpu.VMEM((8, 64, HEAD), BF16),
            pltpu.VMEM((8, 64, HEAD), BF16),
            pltpu.VMEM((4, 8, 32, HEAD), BF16),
            pltpu.SemaphoreType.DMA((10,)),
            pltpu.SemaphoreType.DMA((6,)),
            pltpu.SemaphoreType.DMA((COPIES,)),
            pltpu.SemaphoreType.DMA((COPIES,)),
        ],
        compiler_params=pltpu.CompilerParams(
            collective_id=0, has_side_effects=True, vmem_limit_bytes=56 * 1024 * 1024
        ),
    )(
        queries,
        keys,
        values,
        output_gradient,
        output_weight,
        adapter_down.T,
        adapter_up,
        positions[None, :],
        block_pair_mask,
    )
    dq, dk, dv, a, b = pl.pallas_call(
        write_kernel,
        out_shape=(
            out((ROWS, HEADS * HEAD), BF16),
            out((ROWS, 2 * HEAD), BF16),
            out((ROWS, 2 * HEAD), BF16),
            out((32, HEADS * HEAD), F32),
            out((32, WIDTH), F32),
        ),
        in_specs=[anywhere] * 5,
        out_specs=(anywhere,) * 5,
        scratch_shapes=[
            pltpu.VMEM((ROWS, HEADS * HEAD), BF16),
            pltpu.VMEM((ROWS, 2 * HEAD), BF16),
            pltpu.VMEM((ROWS, 2 * HEAD), BF16),
            pltpu.VMEM((32, HEADS * HEAD), F32),
            pltpu.VMEM((4, 8, 32, HEAD), BF16),
            pltpu.VMEM((32, WIDTH), F32),
            pltpu.SemaphoreType.DMA((8,)),
            pltpu.SemaphoreType.DMA((8,)),
        ],
    )(dq, dk, dv, a, b)
    return dq, dk, dv, a.T, b


def solution(mesh):
    placed = (
        P("seq", "rep"),
        P("seq", "rep"),
        P("seq", "rep"),
        P("seq", None),
        P("rep", None),
        P("rep", None),
        P(),
        P("seq"),
        P("seq", None, None, None),
    )
    return jax.shard_map(
        shards,
        mesh=mesh,
        in_specs=placed,
        out_specs=(P("seq", "rep"), P("seq", "rep"), P("seq", "rep"), P("rep", None), P()),
        check_vma=False,
    )
```

```python
import jax
import jax.numpy as jnp
import numpy as np
from jax import lax
from jax.experimental import pallas as pl
from jax.experimental.pallas import tpu as pltpu
from jax.sharding import PartitionSpec as P

HEAD = 128
ROWS = 512
HALF = 256
HEADS = 8
WIDTH = 4096
MESH = pl.DeviceIdType.MESH
F32 = jnp.float32
BF16 = jnp.bfloat16
SCALE = HEAD**-0.5
POWER = SCALE * 1.4426950408889634
HIDDEN = -1e30
AT_ONCE = 4
FREQUENCY = [float(np.float32(1000000.0 ** (-i * 2.0 / 128))) for i in range(64)]

K_NEXT, V_NEXT, MID, RS1A, RS1B, ALLJ, AG2, BACK, AG3, COPIES = 0, 2, 4, 8, 16, 24, 32, 40, 42, 74


def dot(a, b):
    return jnp.dot(a, b, preferred_element_type=F32)


def dot_nt(a, b):
    return lax.dot_general(a, b, (((1,), (1,)), ((), ())), preferred_element_type=F32)


def seq_at(j, z):
    return (j // 4) * 32 + z * 4 + j % 4


def layer_kernel(
    q_hbm, k_hbm, v_hbm, og_hbm, w_hbm, down_hbm, up_hbm, pos_hbm, codes_hbm,
    dq_hbm, dk_hbm, dv_hbm, a_hbm, b_hbm,
    pos_row, codes, k_nat, up, down_t, angle, dq_out, dk_out, dv_out, a_out,
    q_nat, og, w, k_all, v_all, k_t, v_t, q_t, diag, weights, stats, attn_own, attn_t, d_attn_t, back_t, down,
    dk_acc, dv_acc, mid_own, mid_all, back_send, back_recv,
    part_a, part_b, rs1a, rs1b, all_j, full, b_all,
    load_sem, store_sem, send_sem, recv_sem,
):
    s, r = lax.axis_index("seq"), lax.axis_index("rep")
    z, j = (s // 4) % 8, (s // 32) * 4 + s % 4
    along_z = [(seq_at(j, (z + o) % 8), r) for o in range(8)]
    along_j = [(seq_at((j + o) % 8, z), r) for o in range(8)]
    along_r = [(s, (r + o) % 4) for o in range(4)]
    after, before = ((s + 1) % 64, r), ((s + 63) % 64, r)
    peers = along_z[1:] + along_j[1:] + along_r[1:] + [after, before]

    def remote(at, src, dst, device):
        return pltpu.make_async_remote_copy(
            src_ref=src, dst_ref=dst, send_sem=send_sem.at[at], recv_sem=recv_sem.at[at],
            device_id=device, device_id_type=MESH,
        )

    def next_v(g):
        return remote(V_NEXT + g, v_all.at[g, 0:ROWS], v_all.at[g, ROWS : 2 * ROWS], after)

    def next_k(g):
        return remote(K_NEXT + g, k_all.at[g, 0:ROWS], k_all.at[g, ROWS : 2 * ROWS], after)

    def mids():
        return [remote(MID + o, mid_own, mid_all.at[o], along_r[o]) for o in range(1, 4)]

    def rs1_a():
        return [
            remote(RS1A + o, part_a.at[(z + o) % 8], rs1a.at[o], along_z[o]) for o in range(1, 8)
        ]

    def rs1_b():
        return [
            remote(RS1B + o, part_b.at[(z + o) % 8], rs1b.at[o], along_z[o]) for o in range(1, 8)
        ]

    def all_j_copies():
        return [remote(ALLJ + o, all_j.at[j], all_j.at[j], along_j[o]) for o in range(1, 8)]

    def ag2(o):
        return remote(AG2 + o, full.at[z], full.at[z], along_z[o])

    def ag3(k):
        block = full.at[(z + 8 - k) % 8, 32:64]
        land = b_all.at[r, (z + 8 - k) % 8]
        return [remote(AG3 + k * 4 + o, block, land, along_r[o]) for o in range(1, 4)]

    def back_copy(g):
        return remote(BACK + g, back_send.at[g], back_recv.at[g], before)

    def begin(copies):
        for copy in copies:
            copy.start()

    def finish(copies):
        for copy in copies:
            copy.wait()

    barrier = pltpu.get_barrier_semaphore()
    for p in peers:
        pl.semaphore_signal(barrier, inc=1, device_id=p, device_id_type=MESH)
    loads = []
    for at, (src, dst) in enumerate([
        (v_hbm.at[:, 0:HEAD], v_all.at[0, 0:ROWS]),
        (v_hbm.at[:, HEAD : 2 * HEAD], v_all.at[1, 0:ROWS]),
        (pos_hbm, pos_row), (codes_hbm, codes), (k_hbm, k_nat), (q_hbm, q_nat), (og_hbm, og), (up_hbm, up), (down_hbm, down_t), (w_hbm, w),
    ]):
        loads.append(pltpu.make_async_copy(src, dst, load_sem.at[at]))
        loads[at].start()
    load_v0, load_v1, load_pos, load_codes, load_k, load_q, load_og, load_up, load_down, load_w = loads

    row = lax.broadcasted_iota(jnp.int32, (64, HEAD), 0)
    freq = jnp.zeros((64, HEAD), F32)
    for i in range(64):
        freq = jnp.where(row == i, FREQUENCY[i], freq)
    load_v0.wait()
    pl.semaphore_wait(barrier, len(peers))
    next_v(0).start()
    load_pos.wait()
    q_pos = pos_row[...].astype(F32)
    phase = freq[:, 0:1] * q_pos
    angle[0] = jnp.cos(phase)
    angle[1] = jnp.sin(phase)
    cosine, sine = angle[0], angle[1]

    def turned(x):
        x1, x2 = x[:64], x[64:]
        return jnp.concatenate([x1 * cosine - x2 * sine, x2 * cosine + x1 * sine], 0)

    load_k.wait()
    for g in range(2):
        k_turned = turned(k_nat[:, g * HEAD : (g + 1) * HEAD].astype(F32).T)
        k_t[g, :, 0:ROWS] = k_turned.astype(BF16)
        k_all[g, 0:ROWS] = k_turned.T.astype(BF16)
        next_k(g).start()
    load_v1.wait()
    next_v(1).start()
    for g in range(2):
        v_t[g, :, 0:ROWS] = v_all[g, 0:ROWS].astype(F32).T.astype(BF16)

    load_codes.wait()
    k_pos = jnp.broadcast_to(q_pos, (8, ROWS)).T[:, 0:1]

    def hidden(step, a, b):
        return jnp.where(codes[0, step, a, b] == 1, 0.0, HIDDEN).astype(F32)

    for a in range(2):
        code = codes[0, 0, a, a]
        early = k_pos[a * HALF : (a + 1) * HALF] <= q_pos[:, a * HALF : (a + 1) * HALF]
        shown = jnp.where(early, jnp.where(code >= 1, 0.0, HIDDEN), jnp.where(code == 1, 0.0, HIDDEN))
        diag[a] = shown.astype(F32)

    load_q.wait()

    def turn_queries(h, carry):
        x = q_nat[:, pl.ds(pl.multiple_of(h * HEAD, HEAD), HEAD)].astype(F32).T
        q_t[h] = turned(x).astype(BF16)
        return carry

    lax.fori_loop(0, HEADS, turn_queries, 0)

    def forward_own(i, carry):
        heads = [i * AT_ONCE + u for u in range(AT_ONCE)]
        g = heads[0] // 4

        raws = [dot(k_all[g, 0:ROWS], q_t[h]) for h in heads]
        rounded = []
        for h, raw in zip(heads, raws):
            columns = []
            for a in range(2):
                cols = slice(a * HALF, (a + 1) * HALF)
                same = raw[cols, cols] + diag[a]
                other = raw[(1 - a) * HALF : (2 - a) * HALF, cols]
                off = hidden(0, a, 1 - a)
                top = jnp.maximum(
                    jnp.max(same, 0, keepdims=True), jnp.max(other, 0, keepdims=True) + off
                )
                shift = top * -POWER
                same = jnp.exp2(same * POWER + shift)
                other = jnp.exp2(other * POWER + (shift + off))
                total = jnp.sum(same, 0, keepdims=True) + jnp.sum(other, 0, keepdims=True)
                stats[h, 0:1, cols] = top
                stats[h, 1:2, cols] = total
                pair = [same, other] if a == 0 else [other, same]
                columns.append(jnp.concatenate(pair, 0).astype(BF16))
            rounded.append(jnp.concatenate(columns, 1))
        for h, e in zip(heads, rounded):
            weights[h, 0:ROWS] = e
            attn_own[h] = dot(v_t[g, :, 0:ROWS], e)
        return carry

    lax.fori_loop(0, HEADS // AT_ONCE, forward_own, 0)

    load_og.wait()
    load_up.wait()
    load_down.wait()
    back_t[...] = dot_nt(up[...], og[...]).astype(BF16)
    down[...] = down_t[...].astype(F32).T.astype(BF16)
    load_w.wait()

    def project(i, carry):
        at = pl.multiple_of(i * 512, 512)
        x = dot_nt(w[pl.ds(at, 512)], og[...]) + 2.0 * dot(down[pl.ds(at, 512)], back_t[...])
        d_attn_t[pl.ds(i * 4, 4)] = x.astype(BF16).reshape(4, HEAD, ROWS)
        return carry

    project(0, 0)

    def previous_scores(g):
        heads = range(g * 4, g * 4 + 4)
        raws = [dot(k_all[g, ROWS : 2 * ROWS], q_t[h]) for h in heads]
        for h, raw in zip(heads, raws):
            columns = []
            for a in range(2):
                cols = slice(a * HALF, (a + 1) * HALF)
                first, second = raw[0:HALF, cols], raw[HALF:ROWS, cols]
                off1, off2 = hidden(1, a, 0), hidden(1, a, 1)
                top = jnp.maximum(
                    jnp.max(first, 0, keepdims=True) + off1, jnp.max(second, 0, keepdims=True) + off2
                )
                shift = jnp.minimum(top * -POWER, 1e28)
                first = jnp.exp2(first * POWER + (shift + off1))
                second = jnp.exp2(second * POWER + (shift + off2))
                total = jnp.sum(first, 0, keepdims=True) + jnp.sum(second, 0, keepdims=True)
                top_own = stats[h, 0:1, cols]
                top_all = jnp.maximum(top, top_own)
                own = jnp.exp2((top_own - top_all) * POWER)
                previous = jnp.exp2((top - top_all) * POWER)
                share = 1.0 / (stats[h, 1:2, cols] * own + total * previous)
                own, previous = own * share, previous * share
                stats[h, 2:3, cols] = own
                stats[h, 3:4, cols] = previous
                columns.append(jnp.concatenate([first, second], 0).astype(BF16))
            weights[h, ROWS : 2 * ROWS] = jnp.concatenate(columns, 1)

    def previous_values(g):
        v_t[g, :, ROWS : 2 * ROWS] = v_all[g, ROWS : 2 * ROWS].astype(F32).T.astype(BF16)
        for h in range(g * 4, g * 4 + 4):
            part = dot(v_t[g, :, ROWS : 2 * ROWS], weights[h, ROWS : 2 * ROWS])
            attn_t[h] = (attn_own[h] * stats[h, 2:3] + part * stats[h, 3:4]).astype(BF16)

    next_k(0).wait()
    next_v(0).wait()
    previous_scores(0)
    previous_values(0)
    next_k(1).wait()
    previous_scores(1)
    next_v(1).wait()
    previous_values(1)

    mid_part = dot(down_t[...], attn_t[...].reshape(HEADS * HEAD, ROWS))
    mid_own[...] = mid_part.astype(BF16)
    begin(mids())
    for h in range(HEADS):
        part_a[h] = dot_nt(back_t[...], attn_t[h]).astype(BF16)
    begin(rs1_a())

    def backward(t, g):
        rows = slice(t * ROWS, (t + 1) * ROWS)
        heads = range(g * 4, g * 4 + 4)
        d_weights = [dot(v_all[g, rows], d_attn_t[h]) for h in heads]
        d_scores, scaled = [], []
        for h, d_weight in zip(heads, d_weights):
            grad = d_attn_t[h].astype(F32)
            factor = stats[h, 2 + t : 3 + t]
            if t == 1:
                stats[h, 4:5] = jnp.sum(grad * attn_t[h].astype(F32), 0, keepdims=True)
            delta = stats[h, 4:5]
            p = weights[h, rows].astype(F32)
            d_scores.append((p * (d_weight * factor - delta * factor)).astype(BF16))
            scaled.append((grad * factor).astype(BF16))
        dk = [dot_nt(x, q_t[h]) for h, x in zip(heads, d_scores)]
        dv = [dot_nt(weights[h, rows], x) for h, x in zip(heads, scaled)]
        dk, dv = sum(dk[1:], dk[0]) * SCALE, sum(dv[1:], dv[0])
        if t == 1:
            back_send[g, 0] = dk.astype(BF16)
            back_send[g, 1] = dv.astype(BF16)
        else:
            dk_acc[g] = dk
            dv_acc[g] = dv
        for h, x in zip(heads, d_scores):
            dq = dot(k_t[g, :, rows], x)
            if t == 1:
                attn_own[h] = dq
            else:
                dq = (dq + attn_own[h]) * SCALE
                x1, x2 = dq[:64], dq[64:]
                dq = jnp.concatenate([x1 * cosine + x2 * sine, x2 * cosine - x1 * sine], 0)
                dq_out[:, h * HEAD : (h + 1) * HEAD] = dq.T.astype(BF16)

    def finish_keys(g):
        back_copy(g).wait()
        x = (dk_acc[g] + back_recv[g, 0].astype(F32)).T
        x1, x2 = x[:64], x[64:]
        x = jnp.concatenate([x1 * cosine + x2 * sine, x2 * cosine - x1 * sine], 0)
        dk_out[:, g * HEAD : (g + 1) * HEAD] = x.T.astype(BF16)
        dv = dv_acc[g] + back_recv[g, 1].astype(F32)
        dv_out[:, g * HEAD : (g + 1) * HEAD] = dv.astype(BF16)

    stores = [
        pltpu.make_async_copy(src, dst, store_sem.at[i])
        for i, (src, dst) in enumerate([
            (dq_out.at[:, 0:512], dq_hbm.at[:, 0:512]),
            (dq_out.at[:, 512:1024], dq_hbm.at[:, 512:1024]),
            (dk_out, dk_hbm), (dv_out, dv_hbm), (a_out, a_hbm),
        ])
    ]

    for g in range(2):
        k_t[g, :, ROWS : 2 * ROWS] = k_all[g, ROWS : 2 * ROWS].astype(F32).T.astype(BF16)
    backward(1, 0)
    back_copy(0).start()
    finish(mids())
    mid = mid_part
    for o in range(1, 4):
        mid = mid + mid_all[o].astype(F32)
    b_part = dot(mid.astype(BF16), og[:, pl.ds(pl.multiple_of(r * 1024, 1024), 1024)])
    for c in range(8):
        part_b[c] = b_part[:, c * HEAD : (c + 1) * HEAD].astype(BF16)
    begin(rs1_b())

    project(1, 0)
    finish(rs1_a())
    finish(rs1_b())
    total_a, total_b = part_a[z].astype(F32), part_b[z].astype(F32)
    for o in range(1, 8):
        total_a = total_a + rs1a[o].astype(F32)
        total_b = total_b + rs1b[o].astype(F32)
    all_j[j, 0:32] = total_a.astype(BF16)
    all_j[j, 32:64] = total_b.astype(BF16)
    begin(all_j_copies())

    backward(1, 1)
    finish(all_j_copies())
    total = all_j[0].astype(F32)
    for o in range(1, 8):
        total = total + all_j[o].astype(F32)
    full[z] = (2.0 * total).astype(BF16)
    begin([ag2(o) for o in range(1, 8)])
    begin(ag3(0))
    back_copy(1).start()

    backward(0, 0)
    stores[0].start()
    for o in range(1, 8):
        ag2(o).wait()
        begin(ag3(o))
    b_all[r] = full[:, 32:64, :]
    for c in range(8):
        a_out[:, c * HEAD : (c + 1) * HEAD] = full[c, 0:32].astype(F32)
    stores[4].start()
    backward(0, 1)
    stores[1].start()
    finish_keys(0)
    finish_keys(1)
    stores[2].start()
    stores[3].start()
    for k in range(8):
        finish(ag3(k))
    store_b = pltpu.make_async_copy(b_all, b_hbm, store_sem.at[5])
    store_b.start()
    finish(stores)
    store_b.wait()


def write_kernel(
    dq, dk, dv, a, b, dq_out, dk_out, dv_out, a_out, b_out,
    dq_in, dk_in, dv_in, a_in, b_in, b_wide, in_sem, out_sem,
):
    quarter = ROWS // 4
    steps = [(dk, dk_in, dk_out), (dv, dv_in, dv_out), (a, a_in, a_out)]
    for i in range(4):
        rows = slice(i * quarter, (i + 1) * quarter)
        steps.append((dq.at[rows], dq_in.at[rows], dq_out.at[rows]))
    loads = [pltpu.make_async_copy(x, y, in_sem.at[i]) for i, (x, y, _) in enumerate(steps)]
    stores = [pltpu.make_async_copy(y, o, out_sem.at[i]) for i, (_, y, o) in enumerate(steps)]
    load_b = pltpu.make_async_copy(b, b_in, in_sem.at[7])
    store_b = pltpu.make_async_copy(b_wide, b_out, out_sem.at[7])
    load_b.start()
    for copy in loads:
        copy.start()
    load_b.wait()
    for p in range(4):
        for c in range(8):
            at = p * 1024 + c * HEAD
            b_wide[:, at : at + HEAD] = b_in[p, c].astype(F32)
    store_b.start()
    for load, store in zip(loads, stores):
        load.wait()
        store.start()
    for copy in stores:
        copy.wait()
    store_b.wait()


def shards(
    queries,
    keys,
    values,
    output_gradient,
    output_weight,
    adapter_down,
    adapter_up,
    positions,
    block_pair_mask,
):
    anywhere = pl.BlockSpec(memory_space=pl.ANY)
    hbm = pl.BlockSpec(memory_space=pl.ANY)
    out = jax.ShapeDtypeStruct
    dq, dk, dv, a, b = pl.pallas_call(
        layer_kernel,
        out_shape=(
            out((ROWS, HEADS * HEAD), BF16),
            out((ROWS, 2 * HEAD), BF16),
            out((ROWS, 2 * HEAD), BF16),
            out((32, HEADS * HEAD), F32),
            out((4, 8, 32, HEAD), BF16),
        ),
        in_specs=[hbm] * 9,
        out_specs=(anywhere,) * 5,
        scratch_shapes=[
            pltpu.VMEM((1, ROWS), jnp.int32),
            pltpu.SMEM((1, 2, 2, 2), jnp.int32),
            pltpu.VMEM((ROWS, 2 * HEAD), BF16),
            pltpu.VMEM((32, WIDTH), BF16),
            pltpu.VMEM((32, HEADS * HEAD), BF16),
            pltpu.VMEM((2, 64, ROWS), F32),
            pltpu.VMEM((ROWS, HEADS * HEAD), BF16),
            pltpu.VMEM((ROWS, 2 * HEAD), BF16),
            pltpu.VMEM((ROWS, 2 * HEAD), BF16),
            pltpu.VMEM((32, HEADS * HEAD), F32),
            pltpu.VMEM((ROWS, HEADS * HEAD), BF16),
            pltpu.VMEM((ROWS, WIDTH), BF16),
            pltpu.VMEM((HEADS * HEAD, WIDTH), BF16),
            pltpu.VMEM((2, 2 * ROWS, HEAD), BF16),
            pltpu.VMEM((2, 2 * ROWS, HEAD), BF16),
            pltpu.VMEM((2, HEAD, 2 * ROWS), BF16),
            pltpu.VMEM((2, HEAD, 2 * ROWS), BF16),
            pltpu.VMEM((HEADS, HEAD, ROWS), BF16),
            pltpu.VMEM((2, HALF, HALF), F32),
            pltpu.VMEM((HEADS, 2 * ROWS, ROWS), BF16),
            pltpu.VMEM((HEADS, 8, ROWS), F32),
            pltpu.VMEM((HEADS, HEAD, ROWS), F32),
            pltpu.VMEM((HEADS, HEAD, ROWS), BF16),
            pltpu.VMEM((HEADS, HEAD, ROWS), BF16),
            pltpu.VMEM((32, ROWS), BF16),
            pltpu.VMEM((HEADS * HEAD, 32), BF16),
            pltpu.VMEM((2, ROWS, HEAD), F32),
            pltpu.VMEM((2, ROWS, HEAD), F32),
            pltpu.VMEM((32, ROWS), BF16),
            pltpu.VMEM((4, 32, ROWS), BF16),
            pltpu.VMEM((2, 2, ROWS, HEAD), BF16),
            pltpu.VMEM((2, 2, ROWS, HEAD), BF16),
            pltpu.VMEM((8, 32, HEAD), BF16),
            pltpu.VMEM((8, 32, HEAD), BF16),
            pltpu.VMEM((8, 32, HEAD), BF16),
            pltpu.VMEM((8, 32, HEAD), BF16),
            pltpu.VMEM((8, 64, HEAD), BF16),
            pltpu.VMEM((8, 64, HEAD), BF16),
            pltpu.VMEM((4, 8, 32, HEAD), BF16),
            pltpu.SemaphoreType.DMA((10,)),
            pltpu.SemaphoreType.DMA((6,)),
            pltpu.SemaphoreType.DMA((COPIES,)),
            pltpu.SemaphoreType.DMA((COPIES,)),
        ],
        compiler_params=pltpu.CompilerParams(
            collective_id=0, has_side_effects=True, vmem_limit_bytes=56 * 1024 * 1024
        ),
    )(
        queries,
        keys,
        values,
        output_gradient,
        output_weight,
        adapter_down.T,
        adapter_up,
        positions[None, :],
        block_pair_mask,
    )
    dq, dk, dv, a, b = pl.pallas_call(
        write_kernel,
        out_shape=(
            out((ROWS, HEADS * HEAD), BF16),
            out((ROWS, 2 * HEAD), BF16),
            out((ROWS, 2 * HEAD), BF16),
            out((32, HEADS * HEAD), F32),
            out((32, WIDTH), F32),
        ),
        in_specs=[anywhere] * 5,
        out_specs=(anywhere,) * 5,
        scratch_shapes=[
            pltpu.VMEM((ROWS, HEADS * HEAD), BF16),
            pltpu.VMEM((ROWS, 2 * HEAD), BF16),
            pltpu.VMEM((ROWS, 2 * HEAD), BF16),
            pltpu.VMEM((32, HEADS * HEAD), F32),
            pltpu.VMEM((4, 8, 32, HEAD), BF16),
            pltpu.VMEM((32, WIDTH), F32),
            pltpu.SemaphoreType.DMA((8,)),
            pltpu.SemaphoreType.DMA((8,)),
        ],
    )(dq, dk, dv, a, b)
    return dq, dk, dv, a.T, b


def solution(mesh):
    placed = (
        P("seq", "rep"),
        P("seq", "rep"),
        P("seq", "rep"),
        P("seq", None),
        P("rep", None),
        P("rep", None),
        P(),
        P("seq"),
        P("seq", None, None, None),
    )
    return jax.shard_map(
        shards,
        mesh=mesh,
        in_specs=placed,
        out_specs=(P("seq", "rep"), P("seq", "rep"), P("seq", "rep"), P("rep", None), P()),
        check_vma=False,
    )
```
